32 devices in a mesh: depth: 16 (over z, y, x), rows: 2 (over core).
Axes of the slice: x: 2, y: 2, z: 4, core: 2. Of those that a mesh axis runs over, the one named last changes fastest.
Arguments:
- substrate: float32 [64, 32, 1024], P('depth', 'rows'), may hold values from 0.2 to 1
- catalyst: float32 [64, 32, 1024], P('depth', 'rows'), may hold values from 0 to 0.5
- feed_rate: float32 [64, 32, 1024], P('depth', 'rows'), may hold values from 0.01 to 0.1
- kill_rate: float32 [64, 32, 1024], P('depth', 'rows'), may hold values from 0.03 to 0.1
- extinction: float32 [64, 32, 1024], P('depth', 'rows'), may hold values from 0.001 to 0.03
- palette: float32 [3, 3], replicated, may hold values from -2 to 2
Outputs:
- new_substrate: float32 [64, 32, 1024], P('depth', 'rows')
- new_catalyst: float32 [64, 32, 1024], P('depth', 'rows')
- image: float32 [4, 32, 1024], P(None, 'rows', 'depth')
The draws below stay inside these ranges and needn't reach their ends.
All inputs are finite; a program needn't handle non-finite values.
Results may differ from the reference program's by a relative error of at most 0.000039.
Values sent between devices are 32-bit elements; how exact they have to be, the bound alone decides.
No kernel may reach another device: no remote copies, remote signals or barrier semaphores. Data moves between devices by JAX's collectives and lax.ppermute only.
A program may use at most 64 MiB of HBM per device.

```python
import math
import jax
import jax.numpy as jnp

COLS = 1024
STEPS = 2
DEPTH = 64
ROWS = 32


def level_of(own_key, extent, split, least, largest):
    level = 1.0
    for position, parts in split:
        heights = jax.random.uniform(jax.random.fold_in(jax.random.fold_in(own_key, 6), position), (parts,), jnp.float32, least / len(split), largest / len(split))
        level = level * jnp.repeat(jnp.exp(heights), extent[position] // parts).reshape((-1,) + (1,) * (len(extent) - 1 - position))
    return level


def setup_inputs(seed: int = 0) -> dict:
    seeds = jax.random.split(jax.random.key(seed), 7)
    substrate = jnp.clip(0.2 + 0.8 * jax.random.uniform(seeds[0], (DEPTH, ROWS, COLS), jnp.float32) ** level_of(seeds[0], (DEPTH, ROWS, COLS), ((0, 16), (1, 2)), -0.2, 0.2), 0.2, 1.0)
    catalyst = jnp.clip(0.5 * jax.random.uniform(seeds[1], (DEPTH, ROWS, COLS), jnp.float32) ** level_of(seeds[1], (DEPTH, ROWS, COLS), ((0, 16), (1, 2)), -0.2, 0.2), 0.0, 0.5)
    feed_rate = jnp.clip(jnp.exp(math.log(0.1) - 2.3025851 * jax.random.uniform(seeds[2], (DEPTH, ROWS, COLS), jnp.float32) ** level_of(seeds[2], (DEPTH, ROWS, COLS), ((0, 16), (1, 2)), -0.2, 0.2)), 0.01, 0.1)
    kill_rate = jnp.clip(jnp.exp(math.log(0.1) - 1.2039728 * jax.random.uniform(seeds[3], (DEPTH, ROWS, COLS), jnp.float32) ** level_of(seeds[3], (DEPTH, ROWS, COLS), ((0, 16), (1, 2)), -0.2, 0.2)), 0.03, 0.1)
    extinction = jnp.clip(jnp.exp(math.log(0.03) - 3.4011973 * jax.random.uniform(seeds[4], (DEPTH, ROWS, COLS), jnp.float32) ** level_of(seeds[4], (DEPTH, ROWS, COLS), ((0, 16), (1, 2)), -0.2, 0.2)), 0.001, 0.03)
    palette = jnp.clip(jax.random.uniform(seeds[5], (3, 3), jnp.float32, -2.0, 2.0), -2.0, 2.0)
    return dict(substrate=substrate, catalyst=catalyst, feed_rate=feed_rate, kill_rate=kill_rate, extinction=extinction, palette=palette)


diffusion_fast = 0.08
diffusion_slow = 0.04
time_step = 2.0


def react(padded, feed, kill):
    center = padded[:, 1:-1, 1:-1]
    column_pad = jnp.pad(center, ((0, 0), (0, 0), (0, 0), (1, 1)))
    laplace = padded[:, 2:, 1:-1] + padded[:, :-2, 1:-1] + padded[:, 1:-1, 2:] + padded[:, 1:-1, :-2]
    laplace = laplace + column_pad[..., 2:] + column_pad[..., :-2] - 6.0 * center
    fed = center[0]
    auto = center[1]
    reaction = fed * auto * auto
    fed_change = diffusion_fast * laplace[0] - reaction + feed * (1.0 - fed)
    auto_change = diffusion_slow * laplace[1] + reaction - (feed + kill) * auto
    return jnp.stack([fed + time_step * fed_change, auto + time_step * auto_change])


def shade(fields, extinction, palette):
    fed = fields[0]
    auto = fields[1]
    passing = jnp.exp(-extinction * (0.25 + 4.0 * auto * auto))
    opacity = 1.0 - passing
    colors = jax.nn.sigmoid(8.0 * palette[:, 0, None, None, None] * (fed - 0.65)[None]
                            + 8.0 * palette[:, 1, None, None, None] * (auto - 0.25)[None]
                            + palette[:, 2, None, None, None])
    return passing, opacity, colors


def reference(substrate, catalyst, feed_rate, kill_rate, extinction, palette):
    fields = jnp.stack([substrate, catalyst])
    for iteration in range(STEPS):
        padded = jnp.pad(fields, ((0, 0), (1, 1), (1, 1), (0, 0)))
        fields = react(padded, feed_rate, kill_rate)
    passing, opacity, colors = shade(fields, extinction, palette)
    cumul = jnp.cumprod(passing, axis=0)
    before = jnp.concatenate([jnp.ones_like(passing[:1]), cumul[:-1]], axis=0)
    weights = before * opacity
    image = jnp.stack([jnp.sum(weights * colors[0], axis=0), jnp.sum(weights * colors[1], axis=0),
                       jnp.sum(weights * colors[2], axis=0), jnp.sum(weights, axis=0)])
    return fields[0], fields[1], image
```

```python
import functools

import jax
import jax.numpy as jnp
from jax import lax
from jax.experimental import pallas as pl
from jax.experimental.pallas import tpu as pltpu
from jax.sharding import PartitionSpec as P

diffusion_fast = 0.08
diffusion_slow = 0.04
time_step = 2.0
reach_fast = time_step * diffusion_fast
reach_slow = time_step * diffusion_slow
LANES = 128
SUBLANES = 8
VMEM = pl.BlockSpec(memory_space=pltpu.VMEM)
SMEM = pl.BlockSpec(memory_space=pltpu.SMEM)
PARAMS = pltpu.CompilerParams(vmem_limit_bytes=24 * 1024 * 1024)


def pairings(axis, other):
    count, width = lax.axis_size(axis), lax.axis_size(other)
    flat = (lambda i, j: i * width + j) if axis == "depth" else (lambda i, j: j * count + i)
    result = []
    for shift in (0, 1):
        pairs = []
        for i in range(count):
            partner = ((i + shift) ^ 1) - shift
            for j in range(width):
                if 0 <= partner < count:
                    pairs.append((flat(i, j), flat(partner, j)))
                elif j ^ 1 < width:
                    pairs.append((flat(i, j), flat(i, j ^ 1)))
        result.append(pairs if count > 2 or shift == 0 else None)
    return result


def paired(value, pairs):
    return lax.ppermute(value, ("depth", "rows"), pairs)


def is_even(axis):
    return lax.rem(lax.axis_index(axis), 2) == 0


def shifted_columns(value):
    width = value.shape[-1]
    column = lax.broadcasted_iota(jnp.int32, value.shape, value.ndim - 1)
    left = jnp.where(column == 0, 0.0, pltpu.roll(value, 1, value.ndim - 1))
    right = jnp.where(column == width - 1, 0.0, pltpu.roll(value, width - 1, value.ndim - 1))
    return left + right


def shifted_rows(value, above, below):
    rows = value.shape[0]
    row = lax.broadcasted_iota(jnp.int32, value.shape, 0)
    upper = jnp.where(row == 0, above, pltpu.roll(value, 1, 0))
    lower = jnp.where(row == rows - 1, below, pltpu.roll(value, rows - 1, 0))
    return upper + lower


def react(fed, auto, fed_near, auto_near, feed, kill):
    reaction = fed * auto * auto
    fed_change = diffusion_fast * (fed_near - 6.0 * fed) - reaction + feed * (1.0 - fed)
    auto_change = diffusion_slow * (auto_near - 6.0 * auto) + reaction - (feed + kill) * auto
    return fed + time_step * fed_change, auto + time_step * auto_change


def first_kernel(s_ref, c_ref, f_ref, k_ref, ps_ref, pc_ref, a_ref, b_ref, *row_refs):
    depth, rows, _ = s_ref.shape
    for layer in range(depth):
        near = []
        for ref in (s_ref, c_ref):
            value = ref[layer]
            total = shifted_rows(value, 0.0, 0.0) + shifted_columns(value)
            if layer > 0:
                total = total + ref[layer - 1]
            if layer < depth - 1:
                total = total + ref[layer + 1]
            near.append(total)
        ps_ref[layer], pc_ref[layer] = react(
            s_ref[layer], c_ref[layer], near[0], near[1], f_ref[layer], k_ref[layer]
        )
    fields = (s_ref, c_ref, ps_ref, pc_ref)
    even = is_even("depth")
    for out, towards_next in ((a_ref, even), (b_ref, jnp.logical_not(even))):
        layer = jnp.where(towards_next, depth - 1, 0)
        for n, ref in enumerate(fields):
            out[n] = ref[layer]
    even = is_even("rows")
    for out, towards_next in zip(row_refs, (even, jnp.logical_not(even))):
        for n, ref in enumerate(fields):
            for layer in range(depth):
                head, tail = ref[layer, 0:1], ref[layer, rows - 1 : rows]
                out[n * depth + layer : n * depth + layer + 1] = jnp.where(towards_next, tail, head)


def sides(axis, refs, read):
    index, count = lax.axis_index(axis), lax.axis_size(axis)
    even = is_even(axis)
    first = read(refs[0])
    second = read(refs[1]) if len(refs) == 2 else 0.0
    before = jnp.where(even, second, first)
    after = jnp.where(even, first, second)
    return jnp.where(index == 0, 0.0, before), jnp.where(index == count - 1, 0.0, after)


def corner_kernel(depth, *refs):
    half = len(refs) - 2
    a_ref, b_ref = refs[half:]
    even = is_even("depth")
    for out, towards_next in ((a_ref, even), (b_ref, jnp.logical_not(even))):
        for n in range(2):
            ends = []
            for layer in (0, depth - 1):
                at = n * depth + layer
                ends.append(sides("rows", refs[:half], lambda ref: ref[at : at + 1]))
            for side in range(2):
                at = 2 * n + side
                out[at : at + 1] = jnp.where(towards_next, ends[1][side], ends[0][side])


def second_kernel(depth_count, row_pairings, *refs):
    s_ref, c_ref, f_ref, k_ref, e_ref, palette, ps_ref, pc_ref = refs[:8]
    far = refs[8:10]
    corners = refs[10:12]
    beside = refs[12 : 12 + row_pairings]
    fed_out, auto_out, part_ref = refs[12 + row_pairings : 15 + row_pairings]
    depth, rows, columns = s_ref.shape
    row = lax.broadcasted_iota(jnp.int32, (rows, columns), 0)

    def with_rows(value, above, below):
        return value + jnp.where(row == 0, above, 0.0) + jnp.where(row == rows - 1, below, 0.0)

    steps = []
    for n, (old, partial, reach) in enumerate(
        ((s_ref, ps_ref, reach_fast), (c_ref, pc_ref, reach_slow))
    ):
        old_far = sides("depth", far, lambda ref: ref[n])
        new_far = sides("depth", far, lambda ref: ref[2 + n])
        corner_rows = [sides("depth", corners, lambda ref: ref[2 * n + side : 2 * n + side + 1]) for side in range(2)]
        corner = [[corner_rows[side][end] for side in range(2)] for end in range(2)]
        old_rows, new_rows = [], []
        for layer in range(depth):
            at = n * depth + layer
            old_rows.append(sides("rows", beside, lambda ref: ref[at : at + 1]))
            at = (2 + n) * depth + layer
            new_rows.append(sides("rows", beside, lambda ref: ref[at : at + 1]))
        edge = (lax.axis_index("depth") > 0, lax.axis_index("depth") < depth_count - 1)
        row_edge = (
            lax.axis_index("rows") > 0,
            lax.axis_index("rows") < lax.axis_size("rows") - 1,
        )
        fields = []
        for layer in range(-1, depth + 1):
            if layer in (-1, depth):
                end = 0 if layer < 0 else 1
                own = old[0 if layer < 0 else depth - 1]
                near = with_rows(own, corner[end][0], corner[end][1])
                fields.append(jnp.where(edge[end], new_far[end] + reach * near, 0.0))
                continue
            near = jnp.where(row == 0, old_rows[layer][0], 0.0) + jnp.where(
                row == rows - 1, old_rows[layer][1], 0.0
            )
            if layer == 0:
                near = near + old_far[0]
            if layer == depth - 1:
                near = near + old_far[1]
            fields.append(partial[layer] + reach * near)
        outside = []
        for layer in range(depth):
            ends = []
            for side in range(2):
                near = old[layer, 0:1] if side == 0 else old[layer, rows - 1 : rows]
                if layer == 0:
                    near = near + corner[0][side]
                if layer == depth - 1:
                    near = near + corner[1][side]
                ends.append(jnp.where(row_edge[side], new_rows[layer][side] + reach * near, 0.0))
            outside.append(ends)
        steps.append((fields, outside))

    gather = [0.0, 0.0, 0.0, 0.0]
    before = None
    for layer in range(depth):
        near = []
        for fields, outside in steps:
            value = fields[layer + 1]
            near.append(
                shifted_rows(value, outside[layer][0], outside[layer][1])
                + shifted_columns(value)
                + (fields[layer] + fields[layer + 2])
            )
        fed, auto = react(
            steps[0][0][layer + 1], steps[1][0][layer + 1], near[0], near[1], f_ref[layer], k_ref[layer]
        )
        fed_out[layer] = fed
        auto_out[layer] = auto
        passing = jnp.exp(-e_ref[layer] * (0.25 + 4.0 * auto * auto))
        opacity = 1.0 - passing
        weight = opacity if before is None else before * opacity
        before = passing if before is None else before * passing
        for channel in range(3):
            level = (
                (8.0 * palette[channel, 0]) * (fed - 0.65)
                + (8.0 * palette[channel, 1]) * (auto - 0.25)
                + palette[channel, 2]
            )
            gather[channel] = gather[channel] + weight / (1.0 + jnp.exp(-level))
        gather[3] = gather[3] + weight

    block = columns // depth_count
    group = packing(rows, block)
    if not group:
        for channel in range(4):
            part_ref[channel] = gather[channel]
        return
    high = rows // group
    lane = lax.broadcasted_iota(jnp.int32, (high, LANES), 1) // block
    for channel in range(4):
        for tile in range(columns // LANES):
            pieces = [
                gather[channel][q * high : (q + 1) * high, tile * LANES : (tile + 1) * LANES]
                for q in range(group)
            ]
            for p in range(group):
                packed = None
                for q in range(group):
                    turn = (q - p) * block % LANES
                    piece = pltpu.roll(pieces[q], turn, 1) if turn else pieces[q]
                    packed = piece if packed is None else jnp.where(lane == q, piece, packed)
                part_ref[tile * group + p, channel * high : (channel + 1) * high] = packed


def packing(rows, block):
    if block >= LANES or LANES % block:
        return 0
    group = LANES // block
    return group if rows % (group * SUBLANES) == 0 else 0


def last_kernel(group, part_ref, image_ref):
    _, rows, block = image_ref.shape
    high = rows // group
    count = part_ref.shape[0]
    total = [part_ref[0, channel * high : (channel + 1) * high] for channel in range(4)]
    before = 1.0 - total[3]
    for n in range(1, count):
        for channel in range(4):
            piece = part_ref[n, channel * high : (channel + 1) * high]
            total[channel] = total[channel] + before * piece
        if n < count - 1:
            before = before * (1.0 - piece)
    for channel in range(4):
        for q in range(group):
            image_ref[channel, q * high : (q + 1) * high] = total[channel][:, q * block : (q + 1) * block]


def body(substrate, catalyst, feed_rate, kill_rate, extinction, palette):
    depth, rows, columns = substrate.shape
    count = lax.axis_size("depth")
    f32 = functools.partial(jax.ShapeDtypeStruct, dtype=jnp.float32)
    whole = f32(substrate.shape)
    along_depth = pairings("depth", "rows")
    if along_depth[1] is None:
        along_depth[1] = along_depth[0]
    along_rows = [pairs for pairs in pairings("rows", "depth") if pairs is not None]

    beam = f32((4, rows, columns))
    strip = f32((4 * depth, columns))
    outs = pl.pallas_call(
        first_kernel,
        out_shape=(whole, whole, beam, beam) + (strip,) * len(along_rows),
        in_specs=[VMEM] * 4,
        out_specs=(VMEM,) * (4 + len(along_rows)),
        compiler_params=PARAMS,
        name="first_step",
    )(substrate, catalyst, feed_rate, kill_rate)
    step_fed, step_auto, *beams = outs[:4]
    far = [paired(value, pairs) for value, pairs in zip(beams, along_depth)]
    beside = [paired(value, pairs) for value, pairs in zip(outs[4:], along_rows)]
    corner = f32((SUBLANES, columns))
    corners = pl.pallas_call(
        functools.partial(corner_kernel, depth),
        out_shape=(corner, corner),
        in_specs=[VMEM] * len(beside),
        out_specs=(VMEM, VMEM),
        compiler_params=PARAMS,
        name="corner_rows",
    )(*beside)
    corners = [paired(value, pairs) for value, pairs in zip(corners, along_depth)]

    block = columns // count
    group = packing(rows, block)
    part = f32((count, 4 * rows // group, LANES) if group else (4, rows, columns))
    fed, auto, part = pl.pallas_call(
        functools.partial(second_kernel, count, len(beside)),
        out_shape=(whole, whole, part),
        in_specs=[VMEM] * 5 + [SMEM] + [VMEM] * (6 + len(beside)),
        out_specs=(VMEM,) * 3,
        compiler_params=PARAMS,
        name="second_step",
    )(substrate, catalyst, feed_rate, kill_rate, extinction, palette, step_fed, step_auto, *far, *corners, *beside)
    if not group:
        part = jnp.transpose(part.reshape(4 * rows, count, block), (1, 0, 2))
    part = lax.all_to_all(part, "depth", 0, 0)
    image = pl.pallas_call(
        functools.partial(last_kernel, group or 1),
        out_shape=f32((4, rows, block)),
        in_specs=[VMEM],
        out_specs=VMEM,
        compiler_params=PARAMS,
        name="front_to_back",
    )(part)
    return fed, auto, image


def solution(mesh):
    cells = P("depth", "rows", None)
    return jax.shard_map(
        body,
        mesh=mesh,
        in_specs=(cells,) * 5 + (P(),),
        out_specs=(cells, cells, P(None, "rows", "depth")),
        check_vma=False,
    )
```

```python
import functools

import jax
import jax.numpy as jnp
from jax import lax
from jax.experimental import pallas as pl
from jax.experimental.pallas import tpu as pltpu
from jax.sharding import PartitionSpec as P

diffusion_fast = 0.08
diffusion_slow = 0.04
time_step = 2.0
reach_fast = time_step * diffusion_fast
reach_slow = time_step * diffusion_slow
LANES = 128
SUBLANES = 8
VMEM = pl.BlockSpec(memory_space=pltpu.VMEM)
SMEM = pl.BlockSpec(memory_space=pltpu.SMEM)
HBM = pl.BlockSpec(memory_space=pltpu.HBM)
PARAMS = pltpu.CompilerParams(vmem_limit_bytes=24 * 1024 * 1024)


def pairings(axis, other):
    count, width = lax.axis_size(axis), lax.axis_size(other)
    flat = (lambda i, j: i * width + j) if axis == "depth" else (lambda i, j: j * count + i)
    result = []
    for shift in (0, 1):
        pairs = []
        for i in range(count):
            partner = ((i + shift) ^ 1) - shift
            for j in range(width):
                if 0 <= partner < count:
                    pairs.append((flat(i, j), flat(partner, j)))
                elif j ^ 1 < width:
                    pairs.append((flat(i, j), flat(i, j ^ 1)))
        result.append(pairs if count > 2 or shift == 0 else None)
    return result


def paired(value, pairs):
    return lax.ppermute(value, ("depth", "rows"), pairs)


def is_even(axis):
    return lax.rem(lax.axis_index(axis), 2) == 0


def shifted_columns(value):
    width = value.shape[-1]
    column = lax.broadcasted_iota(jnp.int32, value.shape, value.ndim - 1)
    left = jnp.where(column == 0, 0.0, pltpu.roll(value, 1, value.ndim - 1))
    right = jnp.where(column == width - 1, 0.0, pltpu.roll(value, width - 1, value.ndim - 1))
    return left + right


def shifted_rows(value, above, below):
    rows = value.shape[0]
    row = lax.broadcasted_iota(jnp.int32, value.shape, 0)
    upper = jnp.where(row == 0, above, pltpu.roll(value, 1, 0))
    lower = jnp.where(row == rows - 1, below, pltpu.roll(value, rows - 1, 0))
    return upper + lower


def react(fed, auto, fed_near, auto_near, feed, kill):
    reaction = fed * auto * auto
    fed_change = diffusion_fast * (fed_near - 6.0 * fed) - reaction + feed * (1.0 - fed)
    auto_change = diffusion_slow * (auto_near - 6.0 * auto) + reaction - (feed + kill) * auto
    return fed + time_step * fed_change, auto + time_step * auto_change


def first_kernel(row_pairings, *refs):
    ps_ref, pc_ref, a_ref, b_ref = refs[4:8]
    row_refs = refs[8 : 8 + row_pairings]
    *held, arrived = refs[8 + row_pairings :]
    copies = [pltpu.make_async_copy(refs[n], held[n], arrived.at[n]) for n in range(4)]
    for copy in copies:
        copy.start()
    for copy in copies:
        copy.wait()
    s_ref, c_ref, f_ref, k_ref = held
    depth, rows, _ = s_ref.shape
    for layer in range(depth):
        near = []
        for ref in (s_ref, c_ref):
            value = ref[layer]
            total = shifted_rows(value, 0.0, 0.0) + shifted_columns(value)
            if layer > 0:
                total = total + ref[layer - 1]
            if layer < depth - 1:
                total = total + ref[layer + 1]
            near.append(total)
        ps_ref[layer], pc_ref[layer] = react(
            s_ref[layer], c_ref[layer], near[0], near[1], f_ref[layer], k_ref[layer]
        )
    fields = (s_ref, c_ref, ps_ref, pc_ref)
    even = is_even("depth")
    for out, towards_next in ((a_ref, even), (b_ref, jnp.logical_not(even))):
        layer = jnp.where(towards_next, depth - 1, 0)
        for n, ref in enumerate(fields):
            out[n] = ref[layer]
    even = is_even("rows")
    for out, towards_next in zip(row_refs, (even, jnp.logical_not(even))):
        for n, ref in enumerate(fields):
            for layer in range(depth):
                head, tail = ref[layer, 0:1], ref[layer, rows - 1 : rows]
                out[n * depth + layer : n * depth + layer + 1] = jnp.where(towards_next, tail, head)


def sides(axis, refs, read):
    index, count = lax.axis_index(axis), lax.axis_size(axis)
    even = is_even(axis)
    first = read(refs[0])
    second = read(refs[1]) if len(refs) == 2 else 0.0
    before = jnp.where(even, second, first)
    after = jnp.where(even, first, second)
    return jnp.where(index == 0, 0.0, before), jnp.where(index == count - 1, 0.0, after)


def corner_kernel(depth, *refs):
    half = len(refs) - 2
    a_ref, b_ref = refs[half:]
    even = is_even("depth")
    for out, towards_next in ((a_ref, even), (b_ref, jnp.logical_not(even))):
        for n in range(2):
            ends = []
            for layer in (0, depth - 1):
                at = n * depth + layer
                ends.append(sides("rows", refs[:half], lambda ref: ref[at : at + 1]))
            for side in range(2):
                at = 2 * n + side
                out[at : at + 1] = jnp.where(towards_next, ends[1][side], ends[0][side])


def second_kernel(depth_count, row_pairings, *refs):
    s_ref, c_ref, f_ref, k_ref, e_ref, palette, ps_ref, pc_ref = refs[:8]
    far = refs[8:10]
    corners = refs[10:12]
    beside = refs[12 : 12 + row_pairings]
    fed_out, auto_out, part_ref = refs[12 + row_pairings : 15 + row_pairings]
    depth, rows, columns = s_ref.shape
    row = lax.broadcasted_iota(jnp.int32, (rows, columns), 0)

    def with_rows(value, above, below):
        return value + jnp.where(row == 0, above, 0.0) + jnp.where(row == rows - 1, below, 0.0)

    steps = []
    for n, (old, partial, reach) in enumerate(
        ((s_ref, ps_ref, reach_fast), (c_ref, pc_ref, reach_slow))
    ):
        old_far = sides("depth", far, lambda ref: ref[n])
        new_far = sides("depth", far, lambda ref: ref[2 + n])
        corner_rows = [sides("depth", corners, lambda ref: ref[2 * n + side : 2 * n + side + 1]) for side in range(2)]
        corner = [[corner_rows[side][end] for side in range(2)] for end in range(2)]
        old_rows, new_rows = [], []
        for layer in range(depth):
            at = n * depth + layer
            old_rows.append(sides("rows", beside, lambda ref: ref[at : at + 1]))
            at = (2 + n) * depth + layer
            new_rows.append(sides("rows", beside, lambda ref: ref[at : at + 1]))
        edge = (lax.axis_index("depth") > 0, lax.axis_index("depth") < depth_count - 1)
        row_edge = (
            lax.axis_index("rows") > 0,
            lax.axis_index("rows") < lax.axis_size("rows") - 1,
        )
        fields = []
        for layer in range(-1, depth + 1):
            if layer in (-1, depth):
                end = 0 if layer < 0 else 1
                own = old[0 if layer < 0 else depth - 1]
                near = with_rows(own, corner[end][0], corner[end][1])
                fields.append(jnp.where(edge[end], new_far[end] + reach * near, 0.0))
                continue
            near = jnp.where(row == 0, old_rows[layer][0], 0.0) + jnp.where(
                row == rows - 1, old_rows[layer][1], 0.0
            )
            if layer == 0:
                near = near + old_far[0]
            if layer == depth - 1:
                near = near + old_far[1]
            fields.append(partial[layer] + reach * near)
        outside = []
        for layer in range(depth):
            ends = []
            for side in range(2):
                near = old[layer, 0:1] if side == 0 else old[layer, rows - 1 : rows]
                if layer == 0:
                    near = near + corner[0][side]
                if layer == depth - 1:
                    near = near + corner[1][side]
                ends.append(jnp.where(row_edge[side], new_rows[layer][side] + reach * near, 0.0))
            outside.append(ends)
        steps.append((fields, outside))

    gather = [0.0, 0.0, 0.0, 0.0]
    before = None
    for layer in range(depth):
        near = []
        for fields, outside in steps:
            value = fields[layer + 1]
            near.append(
                shifted_rows(value, outside[layer][0], outside[layer][1])
                + shifted_columns(value)
                + (fields[layer] + fields[layer + 2])
            )
        fed, auto = react(
            steps[0][0][layer + 1], steps[1][0][layer + 1], near[0], near[1], f_ref[layer], k_ref[layer]
        )
        fed_out[layer] = fed
        auto_out[layer] = auto
        passing = jnp.exp(-e_ref[layer] * (0.25 + 4.0 * auto * auto))
        opacity = 1.0 - passing
        weight = opacity if before is None else before * opacity
        before = passing if before is None else before * passing
        for channel in range(3):
            level = (
                (8.0 * palette[channel, 0]) * (fed - 0.65)
                + (8.0 * palette[channel, 1]) * (auto - 0.25)
                + palette[channel, 2]
            )
            gather[channel] = gather[channel] + weight / (1.0 + jnp.exp(-level))
        gather[3] = gather[3] + weight

    block = columns // depth_count
    group = packing(rows, block)
    if not group:
        for channel in range(4):
            part_ref[channel] = gather[channel]
        return
    high = rows // group
    lane = lax.broadcasted_iota(jnp.int32, (high, LANES), 1) // block
    for channel in range(4):
        for tile in range(columns // LANES):
            pieces = [
                gather[channel][q * high : (q + 1) * high, tile * LANES : (tile + 1) * LANES]
                for q in range(group)
            ]
            for p in range(group):
                packed = None
                for q in range(group):
                    turn = (q - p) * block % LANES
                    piece = pltpu.roll(pieces[q], turn, 1) if turn else pieces[q]
                    packed = piece if packed is None else jnp.where(lane == q, piece, packed)
                part_ref[tile * group + p, channel * high : (channel + 1) * high] = packed


def packing(rows, block):
    if block >= LANES or LANES % block:
        return 0
    group = LANES // block
    return group if rows % (group * SUBLANES) == 0 else 0


def last_kernel(group, part_ref, image_ref):
    _, rows, block = image_ref.shape
    high = rows // group
    count = part_ref.shape[0]
    total = [part_ref[0, channel * high : (channel + 1) * high] for channel in range(4)]
    before = 1.0 - total[3]
    for n in range(1, count):
        for channel in range(4):
            piece = part_ref[n, channel * high : (channel + 1) * high]
            total[channel] = total[channel] + before * piece
        if n < count - 1:
            before = before * (1.0 - piece)
    for channel in range(4):
        for q in range(group):
            image_ref[channel, q * high : (q + 1) * high] = total[channel][:, q * block : (q + 1) * block]


def body(substrate, catalyst, feed_rate, kill_rate, extinction, palette):
    depth, rows, columns = substrate.shape
    count = lax.axis_size("depth")
    f32 = functools.partial(jax.ShapeDtypeStruct, dtype=jnp.float32)
    whole = f32(substrate.shape)
    along_depth = pairings("depth", "rows")
    if along_depth[1] is None:
        along_depth[1] = along_depth[0]
    along_rows = [pairs for pairs in pairings("rows", "depth") if pairs is not None]

    beam = f32((4, rows, columns))
    strip = f32((4 * depth, columns))
    outs = pl.pallas_call(
        functools.partial(first_kernel, len(along_rows)),
        out_shape=(whole, whole, beam, beam) + (strip,) * len(along_rows),
        in_specs=[HBM] * 4,
        out_specs=(VMEM,) * (4 + len(along_rows)),
        scratch_shapes=[pltpu.VMEM(whole.shape, jnp.float32)] * 4 + [pltpu.SemaphoreType.DMA((4,))],
        compiler_params=PARAMS,
        name="first_step",
    )(*(pltpu.with_memory_space_constraint(x, pltpu.HBM) for x in (substrate, catalyst, feed_rate, kill_rate)))
    step_fed, step_auto, *beams = outs[:4]
    far_b = paired(beams[1], along_depth[1])
    far_a = paired(beams[0], along_depth[0])
    far = [far_a, far_b]
    beside = [paired(value, pairs) for value, pairs in zip(outs[4:], along_rows)]
    corner = f32((4, columns))
    corners = pl.pallas_call(
        functools.partial(corner_kernel, depth),
        out_shape=(corner, corner),
        in_specs=[VMEM] * len(beside),
        out_specs=(VMEM, VMEM),
        compiler_params=PARAMS,
        name="corner_rows",
    )(*beside)
    corners = [paired(value, pairs) for value, pairs in zip(corners, along_depth)]

    block = columns // count
    group = packing(rows, block)
    part = f32((count, 4 * rows // group, LANES) if group else (4, rows, columns))
    fed, auto, part = pl.pallas_call(
        functools.partial(second_kernel, count, len(beside)),
        out_shape=(whole, whole, part),
        in_specs=[VMEM] * 5 + [SMEM] + [VMEM] * (6 + len(beside)),
        out_specs=(VMEM,) * 3,
        compiler_params=PARAMS,
        name="second_step",
    )(substrate, catalyst, feed_rate, kill_rate, extinction, palette, step_fed, step_auto, *far, *corners, *beside)
    if not group:
        part = jnp.transpose(part.reshape(4 * rows, count, block), (1, 0, 2))
    part = lax.all_to_all(part, "depth", 0, 0)
    image = pl.pallas_call(
        functools.partial(last_kernel, group or 1),
        out_shape=f32((4, rows, block)),
        in_specs=[VMEM],
        out_specs=VMEM,
        compiler_params=PARAMS,
        name="front_to_back",
    )(part)
    return fed, auto, image


def solution(mesh):
    cells = P("depth", "rows", None)
    return jax.shard_map(
        body,
        mesh=mesh,
        in_specs=(cells,) * 5 + (P(),),
        out_specs=(cells, cells, P(None, "rows", "depth")),
        check_vma=False,
    )
```

```python
import functools

import jax
import jax.numpy as jnp
from jax import lax
from jax.experimental import pallas as pl
from jax.experimental.pallas import tpu as pltpu
from jax.sharding import PartitionSpec as P

diffusion_fast = 0.08
diffusion_slow = 0.04
time_step = 2.0
reach_fast = time_step * diffusion_fast
reach_slow = time_step * diffusion_slow
LANES = 128
SUBLANES = 8
VMEM = pl.BlockSpec(memory_space=pltpu.VMEM)
SMEM = pl.BlockSpec(memory_space=pltpu.SMEM)
HBM = pl.BlockSpec(memory_space=pltpu.HBM)
WORK = pl.CostEstimate(flops=20_000_000, bytes_accessed=4_000_000, transcendentals=0)
PARAMS = pltpu.CompilerParams(vmem_limit_bytes=24 * 1024 * 1024)


def pairings(axis, other):
    count, width = lax.axis_size(axis), lax.axis_size(other)
    flat = (lambda i, j: i * width + j) if axis == "depth" else (lambda i, j: j * count + i)
    result = []
    for shift in (0, 1):
        pairs = []
        for i in range(count):
            partner = ((i + shift) ^ 1) - shift
            for j in range(width):
                if 0 <= partner < count:
                    pairs.append((flat(i, j), flat(partner, j)))
                elif j ^ 1 < width:
                    pairs.append((flat(i, j), flat(i, j ^ 1)))
        result.append(pairs if count > 2 or shift == 0 else None)
    return result


def paired(value, pairs):
    return lax.ppermute(value, ("depth", "rows"), pairs)


def is_even(axis):
    return lax.rem(lax.axis_index(axis), 2) == 0


def shifted_columns(value):
    width = value.shape[-1]
    column = lax.broadcasted_iota(jnp.int32, value.shape, value.ndim - 1)
    left = jnp.where(column == 0, 0.0, pltpu.roll(value, 1, value.ndim - 1))
    right = jnp.where(column == width - 1, 0.0, pltpu.roll(value, width - 1, value.ndim - 1))
    return left + right


def shifted_rows(value, above, below):
    rows = value.shape[0]
    row = lax.broadcasted_iota(jnp.int32, value.shape, 0)
    upper = jnp.where(row == 0, above, pltpu.roll(value, 1, 0))
    lower = jnp.where(row == rows - 1, below, pltpu.roll(value, rows - 1, 0))
    return upper + lower


def react(fed, auto, fed_near, auto_near, feed, kill):
    reaction = fed * auto * auto
    fed_change = diffusion_fast * (fed_near - 6.0 * fed) - reaction + feed * (1.0 - fed)
    auto_change = diffusion_slow * (auto_near - 6.0 * auto) + reaction - (feed + kill) * auto
    return fed + time_step * fed_change, auto + time_step * auto_change


def partial_step(s_ref, c_ref, feed, kill, layer, inner):
    near = []
    for ref in (s_ref, c_ref):
        value = ref[layer]
        total = shifted_rows(value, 0.0, 0.0) + shifted_columns(value)
        for other in inner:
            total = total + ref[other]
        near.append(total)
    return react(s_ref[layer], c_ref[layer], near[0], near[1], feed, kill)


def beam_kernel(s_hbm, c_hbm, f_hbm, k_hbm, a_ref, b_ref, s_ref, c_ref, f_ref, k_ref, arrived):
    depth = s_hbm.shape[0]
    even = is_even("depth")
    ends = []
    for n, towards_next in enumerate((even, jnp.logical_not(even))):
        layer = jnp.where(towards_next, depth - 1, 0)
        places = [layer]
        if depth > 1:
            places.append(jnp.where(towards_next, depth - 2, 1))
        copies = []
        for m, place in enumerate(places):
            for i, (hbm, ref) in enumerate(((s_hbm, s_ref), (c_hbm, c_ref))):
                copies.append(pltpu.make_async_copy(hbm.at[place], ref.at[2 * n + m], arrived.at[n, 2 * m + i]))
        for i, (hbm, ref) in enumerate(((f_hbm, f_ref), (k_hbm, k_ref))):
            copies.append(pltpu.make_async_copy(hbm.at[layer], ref.at[n], arrived.at[n, 4 + i]))
        for copy in copies:
            copy.start()
        ends.append(copies)
    for n, out in enumerate((a_ref, b_ref)):
        for copy in ends[n]:
            copy.wait()
        out[0] = s_ref[2 * n]
        out[1] = c_ref[2 * n]
        inner = [2 * n + 1] if depth > 1 else []
        out[2], out[3] = partial_step(s_ref, c_ref, f_ref[n], k_ref[n], 2 * n, inner)


def strip_kernel(s_ref, c_ref, f_ref, k_ref, ps_ref, pc_ref, *strips):
    depth, rows, _ = s_ref.shape
    for layer in range(depth):
        inner = [other for other in (layer - 1, layer + 1) if 0 <= other < depth]
        ps_ref[layer], pc_ref[layer] = partial_step(s_ref, c_ref, f_ref[layer], k_ref[layer], layer, inner)
    even = is_even("rows")
    for out, towards_next in zip(strips, (even, jnp.logical_not(even))):
        for n, ref in enumerate((s_ref, c_ref, ps_ref, pc_ref)):
            for layer in range(depth):
                head, tail = ref[layer, 0:1], ref[layer, rows - 1 : rows]
                out[n * depth + layer : n * depth + layer + 1] = jnp.where(towards_next, tail, head)


def sides(axis, refs, read):
    index, count = lax.axis_index(axis), lax.axis_size(axis)
    even = is_even(axis)
    first = read(refs[0])
    second = read(refs[1]) if len(refs) == 2 else 0.0
    before = jnp.where(even, second, first)
    after = jnp.where(even, first, second)
    return jnp.where(index == 0, 0.0, before), jnp.where(index == count - 1, 0.0, after)


def step_two(fields, outside, layer, others, feed, kill):
    near = []
    for n in range(2):
        value = fields[n][layer]
        total = shifted_rows(value, outside[n][layer][0], outside[n][layer][1]) + shifted_columns(value)
        for other in others[n]:
            total = total + other
        near.append(total)
    return react(fields[0][layer], fields[1][layer], near[0], near[1], feed, kill)


def inner_kernel(s_ref, c_ref, f_ref, k_ref, e_ref, ps_ref, pc_ref, *refs):
    *beside, fed_one, auto_one, fed_two, auto_two, outer_ref, fade_ref = refs
    depth, rows, columns = s_ref.shape
    row = lax.broadcasted_iota(jnp.int32, (rows, columns), 0)
    index, last = lax.axis_index("rows"), lax.axis_size("rows") - 1
    inside = (index > 0, index < last)
    fields, outside = [], []
    for n, (old, partial, out, reach) in enumerate(
        ((s_ref, ps_ref, fed_one, reach_fast), (c_ref, pc_ref, auto_one, reach_slow))
    ):
        values, rows_outside = [], []
        for layer in range(depth):
            at = n * depth + layer
            above, below = sides("rows", beside, lambda ref: ref[at : at + 1])
            near = jnp.where(row == 0, above, 0.0) + jnp.where(row == rows - 1, below, 0.0)
            value = partial[layer] + reach * near
            values.append(value)
            out[layer] = value
            at = (2 + n) * depth + layer
            beyond = sides("rows", beside, lambda ref: ref[at : at + 1])
            ends = []
            for side, own in enumerate((old[layer, 0:1], old[layer, rows - 1 : rows])):
                end = jnp.where(inside[side], beyond[side] + reach * own, 0.0)
                ends.append(end)
                at = (n * 2 + side) * depth + layer
                outer_ref[at : at + 1] = end
            rows_outside.append(ends)
        fields.append(values)
        outside.append(rows_outside)
    for layer in range(1, depth - 1):
        others = [(values[layer - 1], values[layer + 1]) for values in fields]
        fed_two[layer], auto_two[layer] = step_two(fields, outside, layer, others, f_ref[layer], k_ref[layer])
    for layer in range(depth):
        fade_ref[layer] = -e_ref[layer]


def corner_kernel(a_ref, b_ref, _, *outs):
    rows = a_ref.shape[1]
    even = is_even("rows")
    for out, towards_next in zip(outs, (even, jnp.logical_not(even))):
        for n in range(2):
            pair = sides(
                "depth",
                (a_ref, b_ref),
                lambda ref: jnp.where(towards_next, ref[n, rows - 1 : rows], ref[n, 0:1]),
            )
            for end in range(2):
                out[2 * n + end : 2 * n + end + 1] = pair[end]


class Shading:
    def __init__(self, palette):
        self.palette = palette
        self.gather = None
        self.before = None

    def put(self, pieces, passing):
        if self.gather is None:
            self.gather, self.before = list(pieces), passing
            return
        self.gather = [total + self.before * piece for total, piece in zip(self.gather, pieces)]
        self.before = self.before * passing

    def add(self, fed, auto, fade):
        passing = jnp.exp(fade * (0.25 + 4.0 * auto * auto))
        opacity = 1.0 - passing
        pieces = []
        for channel in range(3):
            level = (
                (8.0 * self.palette[channel, 0]) * (fed - 0.65)
                + (8.0 * self.palette[channel, 1]) * (auto - 0.25)
                + self.palette[channel, 2]
            )
            pieces.append(opacity / (1.0 + jnp.exp(-level)))
        self.put(pieces + [opacity], passing)


def second_kernel(*refs):
    s_ref, c_ref, f_ref, k_ref, fade_ref, palette = refs[:6]
    fed_one, auto_one, fed_mid, auto_mid, outer_ref = refs[6:11]
    far = refs[11:13]
    fed_two, auto_two, middle_ref = refs[13:]
    depth = s_ref.shape[0]
    index, last = lax.axis_index("depth"), lax.axis_size("depth") - 1
    inside = (index > 0, index < last)
    fields, outside, beyond, far_old = [], [], [], []
    for n, (old, one, reach) in enumerate(((s_ref, fed_one, reach_fast), (c_ref, auto_one, reach_slow))):
        old_far = sides("depth", far, lambda ref: ref[n])
        new_far = sides("depth", far, lambda ref: ref[2 + n])
        far_old.append(old_far)
        beyond.append(
            [
                jnp.where(inside[end], new_far[end] + reach * old[layer], 0.0)
                for end, layer in enumerate((0, depth - 1))
            ]
        )
        values, rows_outside = {}, {}
        for layer in (0, depth - 1):
            near = 0.0
            if layer == 0:
                near = near + old_far[0]
            if layer == depth - 1:
                near = near + old_far[1]
            values[layer] = one[layer] + reach * near
            rows_outside[layer] = [
                outer_ref[(n * 2 + side) * depth + layer : (n * 2 + side) * depth + layer + 1] for side in range(2)
            ]
        fields.append(values)
        outside.append(rows_outside)
    shading = Shading(palette)
    for layer in range(depth):
        if layer in (0, depth - 1):
            others = []
            for n, one in enumerate((fed_one, auto_one)):
                others.append(
                    [
                        beyond[n][0] if layer == 0 else fields[n].get(layer - 1, one[layer - 1]),
                        beyond[n][1] if layer == depth - 1 else fields[n].get(layer + 1, one[layer + 1]),
                    ]
                )
            fed, auto = step_two(fields, outside, layer, others, f_ref[layer], k_ref[layer])
        else:
            fed, auto = fed_mid[layer], auto_mid[layer]
            for end, beside in enumerate((1, depth - 2)):
                if layer == beside:
                    fed = fed + (reach_fast * reach_fast) * far_old[0][end]
                    auto = auto + (reach_slow * reach_slow) * far_old[1][end]
            shading.add(fed, auto, fade_ref[layer])
        fed_two[layer] = fed
        auto_two[layer] = auto
    if shading.gather is not None:
        for n, value in enumerate(shading.gather + [shading.before]):
            middle_ref[n] = value


def shade_kernel(depth_count, fed_two, auto_two, fade_ref, palette, middle_ref, *refs):
    *corners, fed_out, auto_out, part_ref = refs
    depth, rows, columns = fed_two.shape
    row = lax.broadcasted_iota(jnp.int32, (rows, columns), 0)
    shading = Shading(palette)
    for layer in range(depth):
        if layer not in (0, depth - 1):
            if layer == 1:
                shading.put([middle_ref[n] for n in range(4)], middle_ref[4])
            continue
        values = []
        for n, (two, out, reach) in enumerate(
            ((fed_two, fed_out, reach_fast), (auto_two, auto_out, reach_slow))
        ):
            value = two[layer]
            for end, place in enumerate((0, depth - 1)):
                if layer == place:
                    at = 2 * n + end
                    above, below = sides("rows", corners, lambda ref: ref[at : at + 1])
                    near = jnp.where(row == 0, above, 0.0) + jnp.where(row == rows - 1, below, 0.0)
                    value = value + (2.0 * reach * reach) * near
            out[layer] = value
            values.append(value)
        shading.add(values[0], values[1], fade_ref[layer])
    gather = shading.gather

    block = columns // depth_count
    group = packing(rows, block)
    if not group:
        for channel in range(4):
            part_ref[channel] = gather[channel]
        return
    high = rows // group
    lane = lax.broadcasted_iota(jnp.int32, (high, LANES), 1) // block
    for channel in range(4):
        for tile in range(columns // LANES):
            pieces = [
                gather[channel][q * high : (q + 1) * high, tile * LANES : (tile + 1) * LANES]
                for q in range(group)
            ]
            for p in range(group):
                packed = None
                for q in range(group):
                    turn = (q - p) * block % LANES
                    piece = pltpu.roll(pieces[q], turn, 1) if turn else pieces[q]
                    packed = piece if packed is None else jnp.where(lane == q, piece, packed)
                part_ref[tile * group + p, channel * high : (channel + 1) * high] = packed


def packing(rows, block):
    if block >= LANES or LANES % block:
        return 0
    group = LANES // block
    return group if rows % (group * SUBLANES) == 0 else 0


def last_kernel(group, part_ref, fed_ref, auto_ref, image_ref, fed_out, auto_out, written):
    copies = [
        pltpu.make_async_copy(ref, out, written.at[n])
        for n, (ref, out) in enumerate(((fed_ref, fed_out), (auto_ref, auto_out)))
    ]
    for copy in copies:
        copy.start()
    _, rows, block = image_ref.shape
    high = rows // group
    count = part_ref.shape[0]
    total = [part_ref[0, channel * high : (channel + 1) * high] for channel in range(4)]
    before = 1.0 - total[3]
    for n in range(1, count):
        for channel in range(4):
            piece = part_ref[n, channel * high : (channel + 1) * high]
            total[channel] = total[channel] + before * piece
        if n < count - 1:
            before = before * (1.0 - piece)
    for channel in range(4):
        for q in range(group):
            image_ref[channel, q * high : (q + 1) * high] = total[channel][:, q * block : (q + 1) * block]
    for copy in copies:
        copy.wait()


def body(substrate, catalyst, feed_rate, kill_rate, extinction, palette):
    depth, rows, columns = substrate.shape
    count = lax.axis_size("depth")
    f32 = functools.partial(jax.ShapeDtypeStruct, dtype=jnp.float32)
    whole = f32(substrate.shape)
    along_depth = pairings("depth", "rows")
    if along_depth[1] is None:
        along_depth[1] = along_depth[0]
    along_rows = [pairs for pairs in pairings("rows", "depth") if pairs is not None]

    cells = (substrate, catalyst, feed_rate, kill_rate)
    beam = f32((4, rows, columns))
    layers = lambda count: pltpu.VMEM((count, rows, columns), jnp.float32)
    held = layers(depth)
    beams = pl.pallas_call(
        beam_kernel,
        out_shape=(beam, beam),
        in_specs=[HBM] * 4,
        out_specs=(VMEM, VMEM),
        scratch_shapes=[layers(4), layers(4), layers(2), layers(2), pltpu.SemaphoreType.DMA((2, 6))],
        compiler_params=PARAMS,
        name="depth_messages",
    )(*(pltpu.with_memory_space_constraint(x, pltpu.HBM) for x in cells))
    far = [paired(value, pairs) for value, pairs in zip(beams, along_depth)]

    strip = f32((4 * depth, columns))
    step_fed, step_auto, *strips = pl.pallas_call(
        strip_kernel,
        out_shape=(whole, whole) + (strip,) * len(along_rows),
        cost_estimate=WORK,
        in_specs=[VMEM] * 4,
        out_specs=(VMEM,) * (2 + len(along_rows)),
        compiler_params=PARAMS,
        name="row_messages",
    )(*cells)
    beside = [paired(value, pairs) for value, pairs in zip(strips, along_rows)]
    *inner, fade = pl.pallas_call(
        inner_kernel,
        out_shape=(whole,) * 4 + (strip, whole),
        cost_estimate=WORK,
        in_specs=[VMEM] * (7 + len(beside)),
        out_specs=(VMEM,) * 6,
        compiler_params=PARAMS,
        name="inner_cells",
    )(*cells, extinction, step_fed, step_auto, *beside)

    corner = f32((4, columns))
    corners = pl.pallas_call(
        corner_kernel,
        out_shape=(corner,) * len(along_rows),
        in_specs=[VMEM] * 2 + [pl.BlockSpec(memory_space=pl.ANY)],
        out_specs=(VMEM,) * len(along_rows),
        compiler_params=PARAMS,
        name="corner_rows",
    )(*far, inner[4])
    corners = [paired(value, pairs) for value, pairs in zip(corners, along_rows)]
    fed, auto, middle = pl.pallas_call(
        second_kernel,
        out_shape=(held, held, f32((5, rows, columns))),
        in_specs=[VMEM] * 5 + [SMEM] + [VMEM] * 7,
        out_specs=(VMEM,) * 3,
        compiler_params=PARAMS,
        name="second_step",
    )(*cells, fade, palette, *inner, *far)

    block = columns // count
    group = packing(rows, block)
    part = f32((count, 4 * rows // group, LANES) if group else (4, rows, columns))
    fed, auto, part = pl.pallas_call(
        functools.partial(shade_kernel, count),
        out_shape=(held, held, part),
        in_specs=[VMEM] * 3 + [SMEM] + [VMEM] * (1 + len(corners)),
        out_specs=(VMEM,) * 3,
        input_output_aliases={0: 0, 1: 1},
        compiler_params=PARAMS,
        name="shading",
    )(fed, auto, fade, palette, middle, *corners)
    if not group:
        part = jnp.transpose(part.reshape(4 * rows, count, block), (1, 0, 2))
    part = lax.all_to_all(part, "depth", 0, 0)
    image, fed, auto = pl.pallas_call(
        functools.partial(last_kernel, group or 1),
        out_shape=(f32((4, rows, block)), whole, whole),
        in_specs=[VMEM] * 3,
        out_specs=(VMEM, HBM, HBM),
        scratch_shapes=[pltpu.SemaphoreType.DMA((2,))],
        compiler_params=PARAMS,
        name="front_to_back",
    )(part, fed, auto)
    return fed, auto, image


def solution(mesh):
    cells = P("depth", "rows", None)
    return jax.shard_map(
        body,
        mesh=mesh,
        in_specs=(cells,) * 5 + (P(),),
        out_specs=(cells, cells, P(None, "rows", "depth")),
        check_vma=False,
    )
```

```python
import functools

import jax
import jax.numpy as jnp
from jax import lax
from jax.experimental import pallas as pl
from jax.experimental.pallas import tpu as pltpu
from jax.sharding import PartitionSpec as P

diffusion_fast = 0.08
diffusion_slow = 0.04
time_step = 2.0
reach_fast = time_step * diffusion_fast
reach_slow = time_step * diffusion_slow
LANES = 128
SUBLANES = 8
VMEM = pl.BlockSpec(memory_space=pltpu.VMEM)
SMEM = pl.BlockSpec(memory_space=pltpu.SMEM)
HBM = pl.BlockSpec(memory_space=pltpu.HBM)
ANY = pl.BlockSpec(memory_space=pl.ANY)
WORK = pl.CostEstimate(flops=20_000_000, bytes_accessed=4_000_000, transcendentals=0)
PARAMS = pltpu.CompilerParams(vmem_limit_bytes=24 * 1024 * 1024)


def pairings(axis, other):
    count, width = lax.axis_size(axis), lax.axis_size(other)
    flat = (lambda i, j: i * width + j) if axis == "depth" else (lambda i, j: j * count + i)
    result = []
    for shift in (0, 1):
        pairs = []
        for i in range(count):
            partner = ((i + shift) ^ 1) - shift
            for j in range(width):
                if 0 <= partner < count:
                    pairs.append((flat(i, j), flat(partner, j)))
                elif j ^ 1 < width:
                    pairs.append((flat(i, j), flat(i, j ^ 1)))
        result.append(pairs if count > 2 or shift == 0 else None)
    return result


def paired(value, pairs):
    return lax.ppermute(value, ("depth", "rows"), pairs)


def is_even(axis):
    return lax.rem(lax.axis_index(axis), 2) == 0


def shifted_columns(value):
    width = value.shape[-1]
    column = lax.broadcasted_iota(jnp.int32, value.shape, value.ndim - 1)
    left = jnp.where(column == 0, 0.0, pltpu.roll(value, 1, value.ndim - 1))
    right = jnp.where(column == width - 1, 0.0, pltpu.roll(value, width - 1, value.ndim - 1))
    return left + right


def shifted_rows(value, above, below):
    rows = value.shape[0]
    row = lax.broadcasted_iota(jnp.int32, value.shape, 0)
    upper = jnp.where(row == 0, above, pltpu.roll(value, 1, 0))
    lower = jnp.where(row == rows - 1, below, pltpu.roll(value, rows - 1, 0))
    return upper + lower


def react(fed, auto, fed_near, auto_near, feed, kill):
    reaction = fed * auto * auto
    fed_change = diffusion_fast * (fed_near - 6.0 * fed) - reaction + feed * (1.0 - fed)
    auto_change = diffusion_slow * (auto_near - 6.0 * auto) + reaction - (feed + kill) * auto
    return fed + time_step * fed_change, auto + time_step * auto_change


def partial_step(s_ref, c_ref, feed, kill, layer, inner):
    near = []
    for ref in (s_ref, c_ref):
        value = ref[layer]
        total = shifted_rows(value, 0.0, 0.0) + shifted_columns(value)
        for other in inner:
            total = total + ref[other]
        near.append(total)
    return react(s_ref[layer], c_ref[layer], near[0], near[1], feed, kill)


def old_kernel(s_hbm, c_hbm, a_ref, b_ref, arrived):
    depth = s_hbm.shape[0]
    even = is_even("depth")
    copies = []
    for n, (out, towards_next) in enumerate(((a_ref, even), (b_ref, jnp.logical_not(even)))):
        layer = jnp.where(towards_next, depth - 1, 0)
        for i, hbm in enumerate((s_hbm, c_hbm)):
            copies.append(pltpu.make_async_copy(hbm.at[layer], out.at[i], arrived.at[n, i]))
    for copy in copies:
        copy.start()
    for copy in copies:
        copy.wait()


def partial_kernel(*refs):
    held = refs[6:11]
    s_ref, c_ref, f_ref, k_ref, _ = held
    ps_ref, pc_ref, a_ref, b_ref, *strips, arrived = refs[11:]
    copies = [pltpu.make_async_copy(refs[n], held[n], arrived.at[n]) for n in range(5)]
    for copy in copies:
        copy.start()
    for copy in copies[:4]:
        copy.wait()
    depth, rows, _ = s_ref.shape
    for layer in range(depth):
        inner = [other for other in (layer - 1, layer + 1) if 0 <= other < depth]
        ps_ref[layer], pc_ref[layer] = partial_step(s_ref, c_ref, f_ref[layer], k_ref[layer], layer, inner)
    even = is_even("depth")
    for out, towards_next in ((a_ref, even), (b_ref, jnp.logical_not(even))):
        layer = jnp.where(towards_next, depth - 1, 0)
        out[0] = ps_ref[layer]
        out[1] = pc_ref[layer]
    even = is_even("rows")
    for out, towards_next in zip(strips, (even, jnp.logical_not(even))):
        for n, ref in enumerate((s_ref, c_ref, ps_ref, pc_ref)):
            for layer in range(depth):
                head, tail = ref[layer, 0:1], ref[layer, rows - 1 : rows]
                out[n * depth + layer : n * depth + layer + 1] = jnp.where(towards_next, tail, head)
    copies[4].wait()


def sides(axis, refs, read):
    index, count = lax.axis_index(axis), lax.axis_size(axis)
    even = is_even(axis)
    first = read(refs[0])
    second = read(refs[1]) if len(refs) == 2 else 0.0
    before = jnp.where(even, second, first)
    after = jnp.where(even, first, second)
    return jnp.where(index == 0, 0.0, before), jnp.where(index == count - 1, 0.0, after)


def step_two(fields, outside, layer, others, feed, kill):
    near = []
    for n in range(2):
        value = fields[n][layer]
        total = shifted_rows(value, outside[n][layer][0], outside[n][layer][1]) + shifted_columns(value)
        for other in others[n]:
            total = total + other
        near.append(total)
    return react(fields[0][layer], fields[1][layer], near[0], near[1], feed, kill)


def inner_kernel(s_ref, c_ref, f_ref, k_ref, ps_ref, pc_ref, palette, *refs):
    *beside, fed_one, auto_one, fed_two, auto_two, outer_ref, mix_ref = refs
    depth, rows, columns = s_ref.shape
    row = lax.broadcasted_iota(jnp.int32, (rows, columns), 0)
    index, last = lax.axis_index("rows"), lax.axis_size("rows") - 1
    inside = (index > 0, index < last)
    fields, outside = [], []
    for n, (old, partial, out, reach) in enumerate(
        ((s_ref, ps_ref, fed_one, reach_fast), (c_ref, pc_ref, auto_one, reach_slow))
    ):
        values, rows_outside = [], []
        for layer in range(depth):
            at = n * depth + layer
            above, below = sides("rows", beside, lambda ref: ref[at : at + 1])
            near = jnp.where(row == 0, above, 0.0) + jnp.where(row == rows - 1, below, 0.0)
            value = partial[layer] + reach * near
            values.append(value)
            out[layer] = value
            at = (2 + n) * depth + layer
            beyond = sides("rows", beside, lambda ref: ref[at : at + 1])
            ends = []
            for side, own in enumerate((old[layer, 0:1], old[layer, rows - 1 : rows])):
                end = jnp.where(inside[side], beyond[side] + reach * own, 0.0)
                ends.append(end)
                at = (n * 2 + side) * depth + layer
                outer_ref[at : at + 1] = end
            rows_outside.append(ends)
        fields.append(values)
        outside.append(rows_outside)
    for layer in range(1, depth - 1):
        others = [(values[layer - 1], values[layer + 1]) for values in fields]
        fed_two[layer], auto_two[layer] = step_two(fields, outside, layer, others, f_ref[layer], k_ref[layer])
    for channel in range(3):
        for n, scale in enumerate((8.0, 8.0, 1.0)):
            at = 3 * channel + n
            mix_ref[at : at + 1] = jnp.full((1, columns), scale * palette[channel, n], jnp.float32)


def corner_kernel(a_ref, b_ref, _, *outs):
    rows = a_ref.shape[1]
    even = is_even("rows")
    for out, towards_next in zip(outs, (even, jnp.logical_not(even))):
        for n in range(2):
            pair = sides(
                "depth",
                (a_ref, b_ref),
                lambda ref: jnp.where(towards_next, ref[n, rows - 1 : rows], ref[n, 0:1]),
            )
            for end in range(2):
                out[2 * n + end : 2 * n + end + 1] = pair[end]


class Shading:
    def __init__(self, mix_ref):
        self.mix = [[mix_ref[3 * k + n : 3 * k + n + 1] for n in range(3)] for k in range(3)]
        self.gather = None
        self.before = None

    def put(self, pieces, passing):
        if self.gather is None:
            self.gather, self.before = list(pieces), passing
            return
        self.gather = [total + self.before * piece for total, piece in zip(self.gather, pieces)]
        self.before = self.before * passing

    def add(self, fed, auto, extinction):
        passing = jnp.exp(-extinction * (0.25 + 4.0 * auto * auto))
        opacity = 1.0 - passing
        pieces = []
        for fed_mix, auto_mix, offset in self.mix:
            level = fed_mix * (fed - 0.65) + auto_mix * (auto - 0.25) + offset
            pieces.append(opacity / (1.0 + jnp.exp(-level)))
        self.put(pieces + [opacity], passing)


def second_kernel(row_pairings, *refs):
    s_ref, c_ref, f_ref, k_ref, e_ref, mix_ref = refs[:6]
    fed_one, auto_one, fed_mid, auto_mid, outer_ref = refs[6:11]
    far = refs[11:13]
    corners = refs[13 : 13 + row_pairings]
    fed_two, auto_two, middle_ref = refs[13 + row_pairings :]
    depth, rows, columns = s_ref.shape
    row = lax.broadcasted_iota(jnp.int32, (rows, columns), 0)
    index, last = lax.axis_index("depth"), lax.axis_size("depth") - 1
    inside = (index > 0, index < last)
    ends = (0, depth - 1)
    fields, outside, beyond, far_old = [], [], [], []
    for n, (old, one, reach) in enumerate(((s_ref, fed_one, reach_fast), (c_ref, auto_one, reach_slow))):
        old_far = sides("depth", far, lambda ref: ref[n])
        far_old.append(old_far)
        beyond.append([])
        values, rows_outside = {}, {}
        for end, layer in enumerate(ends):
            at = 2 * n + end
            above, below = sides("rows", corners, lambda ref: ref[at : at + 1])
            corner = jnp.where(row == 0, above, 0.0) + jnp.where(row == rows - 1, below, 0.0)
            beyond[n].append(jnp.where(inside[end], reach * old[layer], 0.0) + (2.0 * reach) * corner)
        for layer in set(ends):
            near = 0.0
            for end in range(2):
                if layer == ends[end]:
                    near = near + old_far[end]
            values[layer] = one[layer] + reach * near
            rows_outside[layer] = [
                outer_ref[(n * 2 + side) * depth + layer : (n * 2 + side) * depth + layer + 1] for side in range(2)
            ]
        fields.append(values)
        outside.append(rows_outside)
    shading = Shading(mix_ref)
    for layer in range(depth):
        if layer in ends:
            others = []
            for n, one in enumerate((fed_one, auto_one)):
                others.append(
                    [
                        beyond[n][0] if layer == 0 else fields[n].get(layer - 1, one[layer - 1]),
                        beyond[n][1] if layer == depth - 1 else fields[n].get(layer + 1, one[layer + 1]),
                    ]
                )
            fed, auto = step_two(fields, outside, layer, others, f_ref[layer], k_ref[layer])
        else:
            fed, auto = fed_mid[layer], auto_mid[layer]
            for end, beside in enumerate((1, depth - 2)):
                if layer == beside:
                    fed = fed + (reach_fast * reach_fast) * far_old[0][end]
                    auto = auto + (reach_slow * reach_slow) * far_old[1][end]
            shading.add(fed, auto, e_ref[layer])
        fed_two[layer] = fed
        auto_two[layer] = auto
    if shading.gather is not None:
        for n, value in enumerate(shading.gather + [shading.before]):
            middle_ref[n] = value


def shade_kernel(depth_count, fed_two, auto_two, e_ref, mix_ref, middle_ref, a_ref, b_ref, fed_out, auto_out, part_ref):
    depth, rows, columns = fed_two.shape
    new_far = [sides("depth", (a_ref, b_ref), lambda ref: ref[n]) for n in range(2)]
    shading = Shading(mix_ref)
    for layer in range(depth):
        fed, auto = fed_two[layer], auto_two[layer]
        if layer in (0, depth - 1):
            for end, place in enumerate((0, depth - 1)):
                if layer == place:
                    fed = fed + reach_fast * new_far[0][end]
                    auto = auto + reach_slow * new_far[1][end]
            shading.add(fed, auto, e_ref[layer])
        elif layer == 1:
            shading.put([middle_ref[n] for n in range(4)], middle_ref[4])
        fed_out[layer] = fed
        auto_out[layer] = auto
    gather = shading.gather

    block = columns // depth_count
    group = packing(rows, block)
    if not group:
        for channel in range(4):
            part_ref[channel] = gather[channel]
        return
    high = rows // group
    lane = lax.broadcasted_iota(jnp.int32, (high, LANES), 1) // block
    for channel in range(4):
        for tile in range(columns // LANES):
            pieces = [
                gather[channel][q * high : (q + 1) * high, tile * LANES : (tile + 1) * LANES]
                for q in range(group)
            ]
            for p in range(group):
                packed = None
                for q in range(group):
                    turn = (q - p) * block % LANES
                    piece = pltpu.roll(pieces[q], turn, 1) if turn else pieces[q]
                    packed = piece if packed is None else jnp.where(lane == q, piece, packed)
                part_ref[tile * group + p, channel * high : (channel + 1) * high] = packed


def packing(rows, block):
    if block >= LANES or LANES % block:
        return 0
    group = LANES // block
    return group if rows % (group * SUBLANES) == 0 else 0


def last_kernel(group, part_ref, fed_ref, auto_ref, image_out, fed_out, auto_out, image_ref, written):
    copies = [
        pltpu.make_async_copy(ref, out, written.at[n])
        for n, (ref, out) in enumerate(((fed_ref, fed_out), (auto_ref, auto_out), (image_ref, image_out)))
    ]
    copies[0].start()
    copies[1].start()
    _, rows, block = image_ref.shape
    high = rows // group
    count = part_ref.shape[0]
    total = [part_ref[0, channel * high : (channel + 1) * high] for channel in range(4)]
    before = 1.0 - total[3]
    for n in range(1, count):
        for channel in range(4):
            piece = part_ref[n, channel * high : (channel + 1) * high]
            total[channel] = total[channel] + before * piece
        if n < count - 1:
            before = before * (1.0 - piece)
    for channel in range(4):
        for q in range(group):
            image_ref[channel, q * high : (q + 1) * high] = total[channel][:, q * block : (q + 1) * block]
    copies[2].start()
    for copy in copies:
        copy.wait()


def body(substrate, catalyst, feed_rate, kill_rate, extinction, palette):
    depth, rows, columns = substrate.shape
    count = lax.axis_size("depth")
    f32 = functools.partial(jax.ShapeDtypeStruct, dtype=jnp.float32)
    whole = f32(substrate.shape)
    along_depth = pairings("depth", "rows")
    if along_depth[1] is None:
        along_depth[1] = along_depth[0]
    along_rows = [pairs for pairs in pairings("rows", "depth") if pairs is not None]

    cells = (substrate, catalyst, feed_rate, kill_rate)
    pair = f32((2, rows, columns))
    in_hbm = lambda x: pltpu.with_memory_space_constraint(x, pltpu.HBM)
    old_beams = pl.pallas_call(
        old_kernel,
        out_shape=(pair, pair),
        in_specs=[HBM] * 2,
        out_specs=(VMEM, VMEM),
        scratch_shapes=[pltpu.SemaphoreType.DMA((2, 2))],
        compiler_params=PARAMS,
        name="old_layers",
    )(in_hbm(substrate), in_hbm(catalyst))
    old_far = [paired(value, pairs) for value, pairs in zip(old_beams, along_depth)]

    strip = f32((4 * depth, columns))
    outs = pl.pallas_call(
        partial_kernel,
        out_shape=(whole,) * 7 + (pair, pair) + (strip,) * len(along_rows),
        in_specs=[HBM] * 5 + [ANY],
        out_specs=(VMEM,) * (9 + len(along_rows)),
        scratch_shapes=[pltpu.SemaphoreType.DMA((5,))],
        cost_estimate=WORK,
        compiler_params=PARAMS,
        name="partial_step",
    )(*(in_hbm(x) for x in cells), in_hbm(extinction), old_beams[0])
    cells, extinction, partial = outs[:4], outs[4], outs[5:7]
    new_far = [paired(value, pairs) for value, pairs in zip(outs[7:9], along_depth)]
    beside = [paired(value, pairs) for value, pairs in zip(outs[9:], along_rows)]
    *inner, mix = pl.pallas_call(
        inner_kernel,
        out_shape=(whole,) * 4 + (strip, f32((9, columns))),
        in_specs=[VMEM] * 6 + [SMEM] + [VMEM] * len(beside),
        out_specs=(VMEM,) * 6,
        cost_estimate=WORK,
        compiler_params=PARAMS,
        name="inner_cells",
    )(*cells, *partial, palette, *beside)

    corner = f32((4, columns))
    corners = pl.pallas_call(
        corner_kernel,
        out_shape=(corner,) * len(along_rows),
        in_specs=[VMEM] * 2 + [ANY],
        out_specs=(VMEM,) * len(along_rows),
        compiler_params=PARAMS,
        name="corner_rows",
    )(*old_far, inner[4])
    corners = [paired(value, pairs) for value, pairs in zip(corners, along_rows)]
    fed, auto, middle = pl.pallas_call(
        functools.partial(second_kernel, len(corners)),
        out_shape=(whole, whole, f32((5, rows, columns))),
        in_specs=[VMEM] * (13 + len(corners)),
        out_specs=(VMEM,) * 3,
        cost_estimate=WORK,
        compiler_params=PARAMS,
        name="second_step",
    )(*cells, extinction, mix, *inner, *old_far, *corners)

    block = columns // count
    group = packing(rows, block)
    held = pltpu.VMEM(whole.shape, jnp.float32)
    fed, auto, part = pl.pallas_call(
        functools.partial(shade_kernel, count),
        out_shape=(held, held, f32((count, 4 * rows // group, LANES) if group else (4, rows, columns))),
        in_specs=[VMEM] * 7,
        out_specs=(VMEM,) * 3,
        compiler_params=PARAMS,
        name="shading",
    )(fed, auto, extinction, mix, middle, *new_far)
    if not group:
        part = jnp.transpose(part.reshape(4 * rows, count, block), (1, 0, 2))
    part = lax.all_to_all(part, "depth", 0, 0)
    image = f32((4, rows, block))
    image, fed, auto = pl.pallas_call(
        functools.partial(last_kernel, group or 1),
        out_shape=(image, whole, whole),
        in_specs=[VMEM] * 3,
        out_specs=(HBM,) * 3,
        scratch_shapes=[pltpu.VMEM(image.shape, jnp.float32), pltpu.SemaphoreType.DMA((3,))],
        compiler_params=PARAMS,
        name="front_to_back",
    )(part, fed, auto)
    return fed, auto, image


def solution(mesh):
    cells = P("depth", "rows", None)
    return jax.shard_map(
        body,
        mesh=mesh,
        in_specs=(cells,) * 5 + (P(),),
        out_specs=(cells, cells, P(None, "rows", "depth")),
        check_vma=False,
    )
```

```python
import functools

import jax
import jax.numpy as jnp
from jax import lax
from jax.experimental import pallas as pl
from jax.experimental.pallas import tpu as pltpu
from jax.sharding import PartitionSpec as P

diffusion_fast = 0.08
diffusion_slow = 0.04
time_step = 2.0
reach_fast = time_step * diffusion_fast
reach_slow = time_step * diffusion_slow
LANES = 128
SUBLANES = 8
VMEM = pl.BlockSpec(memory_space=pltpu.VMEM)
SMEM = pl.BlockSpec(memory_space=pltpu.SMEM)
HBM = pl.BlockSpec(memory_space=pltpu.HBM)
ANY = pl.BlockSpec(memory_space=pl.ANY)
WORK = pl.CostEstimate(flops=20_000_000, bytes_accessed=4_000_000, transcendentals=0)
PARAMS = pltpu.CompilerParams(vmem_limit_bytes=24 * 1024 * 1024)


def pairings(axis, other):
    count, width = lax.axis_size(axis), lax.axis_size(other)
    flat = (lambda i, j: i * width + j) if axis == "depth" else (lambda i, j: j * count + i)
    result = []
    for shift in (0, 1):
        pairs = []
        for i in range(count):
            partner = ((i + shift) ^ 1) - shift
            for j in range(width):
                if 0 <= partner < count:
                    pairs.append((flat(i, j), flat(partner, j)))
                elif j ^ 1 < width:
                    pairs.append((flat(i, j), flat(i, j ^ 1)))
        result.append(pairs if count > 2 or shift == 0 else None)
    return result


def paired(value, pairs):
    return lax.ppermute(value, ("depth", "rows"), pairs)


def is_even(axis):
    return lax.rem(lax.axis_index(axis), 2) == 0


def shifted_columns(value):
    width = value.shape[-1]
    column = lax.broadcasted_iota(jnp.int32, value.shape, value.ndim - 1)
    left = jnp.where(column == 0, 0.0, pltpu.roll(value, 1, value.ndim - 1))
    right = jnp.where(column == width - 1, 0.0, pltpu.roll(value, width - 1, value.ndim - 1))
    return left + right


def shifted_rows(value, above, below):
    rows = value.shape[0]
    row = lax.broadcasted_iota(jnp.int32, value.shape, 0)
    upper = jnp.where(row == 0, above, pltpu.roll(value, 1, 0))
    lower = jnp.where(row == rows - 1, below, pltpu.roll(value, rows - 1, 0))
    return upper + lower


def react(fed, auto, fed_near, auto_near, feed, kill):
    reaction = fed * auto * auto
    fed_change = diffusion_fast * (fed_near - 6.0 * fed) - reaction + feed * (1.0 - fed)
    auto_change = diffusion_slow * (auto_near - 6.0 * auto) + reaction - (feed + kill) * auto
    return fed + time_step * fed_change, auto + time_step * auto_change


def partial_step(s_ref, c_ref, feed, kill, layer, inner):
    near = []
    for ref in (s_ref, c_ref):
        value = ref[layer]
        total = shifted_rows(value, 0.0, 0.0) + shifted_columns(value)
        for other in inner:
            total = total + ref[other]
        near.append(total)
    return react(s_ref[layer], c_ref[layer], near[0], near[1], feed, kill)


def old_kernel(s_hbm, c_hbm, palette_hbm, *refs):
    b_ref, a_ref, mix_ref, palette, arrived = refs[-5:]
    depth, _, columns = s_hbm.shape
    even = is_even("depth")
    copies = []
    for n, (out, towards_next) in enumerate(((a_ref, even), (b_ref, jnp.logical_not(even)))):
        layer = jnp.where(towards_next, depth - 1, 0)
        for i, hbm in enumerate((s_hbm, c_hbm)):
            copies.append(pltpu.make_async_copy(hbm.at[layer], out.at[i], arrived.at[n, i]))
    copies.append(pltpu.make_async_copy(palette_hbm, palette, arrived.at[2, 0]))
    for copy in copies:
        copy.start()
    copies[-1].wait()
    for channel in range(3):
        for n, scale in enumerate((8.0, 8.0, 1.0)):
            at = 3 * channel + n
            mix_ref[at : at + 1] = jnp.full((1, columns), scale * palette[channel, n], jnp.float32)
    for copy in copies[:-1]:
        copy.wait()


def partial_kernel(s_ref, c_ref, f_ref, k_ref, _, ps_ref, pc_ref, a_ref, b_ref, *strips):
    depth, rows, _ = s_ref.shape
    for layer in range(depth):
        inner = [other for other in (layer - 1, layer + 1) if 0 <= other < depth]
        ps_ref[layer], pc_ref[layer] = partial_step(s_ref, c_ref, f_ref[layer], k_ref[layer], layer, inner)
    even = is_even("depth")
    for out, towards_next in ((a_ref, even), (b_ref, jnp.logical_not(even))):
        layer = jnp.where(towards_next, depth - 1, 0)
        out[0] = ps_ref[layer]
        out[1] = pc_ref[layer]
    even = is_even("rows")
    for out, towards_next in zip(strips, (even, jnp.logical_not(even))):
        for n, ref in enumerate((s_ref, c_ref, ps_ref, pc_ref)):
            for layer in range(depth):
                head, tail = ref[layer, 0:1], ref[layer, rows - 1 : rows]
                out[n * depth + layer : n * depth + layer + 1] = jnp.where(towards_next, tail, head)


def sides(axis, refs, read):
    index, count = lax.axis_index(axis), lax.axis_size(axis)
    even = is_even(axis)
    first = read(refs[0])
    second = read(refs[1]) if len(refs) == 2 else 0.0
    before = jnp.where(even, second, first)
    after = jnp.where(even, first, second)
    return jnp.where(index == 0, 0.0, before), jnp.where(index == count - 1, 0.0, after)


def step_two(fields, outside, layer, others, feed, kill):
    near = []
    for n in range(2):
        value = fields[n][layer]
        total = shifted_rows(value, outside[n][layer][0], outside[n][layer][1]) + shifted_columns(value)
        for other in others[n]:
            total = total + other
        near.append(total)
    return react(fields[0][layer], fields[1][layer], near[0], near[1], feed, kill)


def inner_kernel(s_ref, c_ref, f_ref, k_ref, ps_ref, pc_ref, *refs):
    *beside, fed_one, auto_one, fed_two, auto_two, outer_ref = refs
    depth, rows, columns = s_ref.shape
    row = lax.broadcasted_iota(jnp.int32, (rows, columns), 0)
    index, last = lax.axis_index("rows"), lax.axis_size("rows") - 1
    inside = (index > 0, index < last)
    fields, outside = [], []
    for n, (old, partial, out, reach) in enumerate(
        ((s_ref, ps_ref, fed_one, reach_fast), (c_ref, pc_ref, auto_one, reach_slow))
    ):
        values, rows_outside = [], []
        for layer in range(depth):
            at = n * depth + layer
            above, below = sides("rows", beside, lambda ref: ref[at : at + 1])
            near = jnp.where(row == 0, above, 0.0) + jnp.where(row == rows - 1, below, 0.0)
            value = partial[layer] + reach * near
            values.append(value)
            out[layer] = value
            at = (2 + n) * depth + layer
            beyond = sides("rows", beside, lambda ref: ref[at : at + 1])
            ends = []
            for side, own in enumerate((old[layer, 0:1], old[layer, rows - 1 : rows])):
                end = jnp.where(inside[side], beyond[side] + reach * own, 0.0)
                ends.append(end)
                at = (n * 2 + side) * depth + layer
                outer_ref[at : at + 1] = end
            rows_outside.append(ends)
        fields.append(values)
        outside.append(rows_outside)
    for layer in range(1, depth - 1):
        others = [(values[layer - 1], values[layer + 1]) for values in fields]
        fed_two[layer], auto_two[layer] = step_two(fields, outside, layer, others, f_ref[layer], k_ref[layer])


def corner_kernel(b_ref, a_ref, _, *outs):
    rows = a_ref.shape[1]
    even = is_even("rows")
    for out, towards_next in zip(outs, (even, jnp.logical_not(even))):
        for n in range(2):
            pair = sides(
                "depth",
                (a_ref, b_ref),
                lambda ref: jnp.where(towards_next, ref[n, rows - 1 : rows], ref[n, 0:1]),
            )
            for end in range(2):
                out[2 * n + end : 2 * n + end + 1] = pair[end]


class Shading:
    def __init__(self, mix_ref):
        self.mix = [[mix_ref[3 * k + n : 3 * k + n + 1] for n in range(3)] for k in range(3)]
        self.gather = None
        self.before = None

    def put(self, pieces, passing):
        if self.gather is None:
            self.gather, self.before = list(pieces), passing
            return
        self.gather = [total + self.before * piece for total, piece in zip(self.gather, pieces)]
        self.before = self.before * passing

    def add(self, fed, auto, extinction):
        passing = jnp.exp(-extinction * (0.25 + 4.0 * auto * auto))
        opacity = 1.0 - passing
        pieces = []
        for fed_mix, auto_mix, offset in self.mix:
            level = fed_mix * (fed - 0.65) + auto_mix * (auto - 0.25) + offset
            pieces.append(opacity / (1.0 + jnp.exp(-level)))
        self.put(pieces + [opacity], passing)


def second_kernel(row_pairings, *refs):
    s_ref, c_ref, f_ref, k_ref, e_ref, mix_ref = refs[:6]
    fed_one, auto_one, fed_mid, auto_mid, outer_ref = refs[6:11]
    far = refs[11:13]
    corners = refs[13 : 13 + row_pairings]
    fed_two, auto_two, middle_ref = refs[13 + row_pairings :]
    depth, rows, columns = s_ref.shape
    row = lax.broadcasted_iota(jnp.int32, (rows, columns), 0)
    index, last = lax.axis_index("depth"), lax.axis_size("depth") - 1
    inside = (index > 0, index < last)
    ends = (0, depth - 1)
    fields, outside, beyond, far_old = [], [], [], []
    for n, (old, one, reach) in enumerate(((s_ref, fed_one, reach_fast), (c_ref, auto_one, reach_slow))):
        old_far = sides("depth", far, lambda ref: ref[n])
        far_old.append(old_far)
        beyond.append([])
        values, rows_outside = {}, {}
        for end, layer in enumerate(ends):
            at = 2 * n + end
            above, below = sides("rows", corners, lambda ref: ref[at : at + 1])
            corner = jnp.where(row == 0, above, 0.0) + jnp.where(row == rows - 1, below, 0.0)
            beyond[n].append(jnp.where(inside[end], reach * old[layer], 0.0) + (2.0 * reach) * corner)
        for layer in set(ends):
            near = 0.0
            for end in range(2):
                if layer == ends[end]:
                    near = near + old_far[end]
            values[layer] = one[layer] + reach * near
            rows_outside[layer] = [
                outer_ref[(n * 2 + side) * depth + layer : (n * 2 + side) * depth + layer + 1] for side in range(2)
            ]
        fields.append(values)
        outside.append(rows_outside)
    shading = Shading(mix_ref)
    for layer in range(depth):
        if layer in ends:
            others = []
            for n, one in enumerate((fed_one, auto_one)):
                others.append(
                    [
                        beyond[n][0] if layer == 0 else fields[n].get(layer - 1, one[layer - 1]),
                        beyond[n][1] if layer == depth - 1 else fields[n].get(layer + 1, one[layer + 1]),
                    ]
                )
            fed, auto = step_two(fields, outside, layer, others, f_ref[layer], k_ref[layer])
        else:
            fed, auto = fed_mid[layer], auto_mid[layer]
            for end, beside in enumerate((1, depth - 2)):
                if layer == beside:
                    fed = fed + (reach_fast * reach_fast) * far_old[0][end]
                    auto = auto + (reach_slow * reach_slow) * far_old[1][end]
            shading.add(fed, auto, e_ref[layer])
        fed_two[layer] = fed
        auto_two[layer] = auto
    if shading.gather is not None:
        for n, value in enumerate(shading.gather + [shading.before]):
            middle_ref[n] = value


def shade_kernel(depth_count, fed_two, auto_two, e_ref, mix_ref, middle_ref, a_ref, b_ref, fed_out, auto_out, part_ref):
    depth, rows, columns = fed_two.shape
    new_far = [sides("depth", (a_ref, b_ref), lambda ref: ref[n]) for n in range(2)]
    shading = Shading(mix_ref)
    for layer in range(depth):
        fed, auto = fed_two[layer], auto_two[layer]
        if layer in (0, depth - 1):
            for end, place in enumerate((0, depth - 1)):
                if layer == place:
                    fed = fed + reach_fast * new_far[0][end]
                    auto = auto + reach_slow * new_far[1][end]
            shading.add(fed, auto, e_ref[layer])
        elif layer == 1:
            shading.put([middle_ref[n] for n in range(4)], middle_ref[4])
        fed_out[layer] = fed
        auto_out[layer] = auto
    gather = shading.gather

    block = columns // depth_count
    group = packing(rows, block)
    if not group:
        for channel in range(4):
            part_ref[channel] = gather[channel]
        return
    high = rows // group
    lane = lax.broadcasted_iota(jnp.int32, (high, LANES), 1) // block
    for channel in range(4):
        for tile in range(columns // LANES):
            pieces = [
                gather[channel][q * high : (q + 1) * high, tile * LANES : (tile + 1) * LANES]
                for q in range(group)
            ]
            for p in range(group):
                packed = None
                for q in range(group):
                    turn = (q - p) * block % LANES
                    piece = pltpu.roll(pieces[q], turn, 1) if turn else pieces[q]
                    packed = piece if packed is None else jnp.where(lane == q, piece, packed)
                part_ref[tile * group + p, channel * high : (channel + 1) * high] = packed


def packing(rows, block):
    if block >= LANES or LANES % block:
        return 0
    group = LANES // block
    return group if rows % (group * SUBLANES) == 0 else 0


def last_kernel(group, part_ref, fed_ref, auto_ref, image_out, fed_out, auto_out, image_ref, written):
    copies = [
        pltpu.make_async_copy(ref, out, written.at[n])
        for n, (ref, out) in enumerate(((fed_ref, fed_out), (auto_ref, auto_out), (image_ref, image_out)))
    ]
    copies[0].start()
    copies[1].start()
    _, rows, block = image_ref.shape
    high = rows // group
    count = part_ref.shape[0]
    total = [part_ref[0, channel * high : (channel + 1) * high] for channel in range(4)]
    before = 1.0 - total[3]
    for n in range(1, count):
        for channel in range(4):
            piece = part_ref[n, channel * high : (channel + 1) * high]
            total[channel] = total[channel] + before * piece
        if n < count - 1:
            before = before * (1.0 - piece)
    for channel in range(4):
        for q in range(group):
            image_ref[channel, q * high : (q + 1) * high] = total[channel][:, q * block : (q + 1) * block]
    copies[2].start()
    for copy in copies:
        copy.wait()


def body(substrate, catalyst, feed_rate, kill_rate, extinction, palette):
    depth, rows, columns = substrate.shape
    count = lax.axis_size("depth")
    f32 = functools.partial(jax.ShapeDtypeStruct, dtype=jnp.float32)
    whole = f32(substrate.shape)
    along_depth = pairings("depth", "rows")
    if along_depth[1] is None:
        along_depth[1] = along_depth[0]
    along_rows = [pairs for pairs in pairings("rows", "depth") if pairs is not None]

    cells = (substrate, catalyst, feed_rate, kill_rate)
    pair = f32((2, rows, columns))
    in_hbm = lambda x: pltpu.with_memory_space_constraint(x, pltpu.HBM)
    *old_beams, mix = pl.pallas_call(
        old_kernel,
        out_shape=(pair, pair, f32((9, columns))),
        in_specs=[HBM] * 6,
        out_specs=(VMEM,) * 3,
        scratch_shapes=[pltpu.SMEM(palette.shape, jnp.float32), pltpu.SemaphoreType.DMA((3, 2))],
        cost_estimate=WORK,
        compiler_params=PARAMS,
        name="old_layers",
    )(*(in_hbm(x) for x in (substrate, catalyst, palette, feed_rate, kill_rate, extinction)))
    old_far = [paired(value, pairs) for value, pairs in zip(old_beams[::-1], along_depth)]

    strip = f32((4 * depth, columns))
    outs = pl.pallas_call(
        partial_kernel,
        out_shape=(whole, whole, pair, pair) + (strip,) * len(along_rows),
        in_specs=[VMEM] * 4 + [ANY],
        out_specs=(VMEM,) * (4 + len(along_rows)),
        cost_estimate=WORK,
        compiler_params=PARAMS,
        name="partial_step",
    )(*cells, old_beams[0])
    partial = outs[:2]
    new_far = [paired(value, pairs) for value, pairs in zip(outs[2:4], along_depth)]
    beside = [paired(value, pairs) for value, pairs in zip(outs[4:], along_rows)]
    inner = pl.pallas_call(
        inner_kernel,
        out_shape=(whole,) * 4 + (strip,),
        in_specs=[VMEM] * (6 + len(beside)),
        out_specs=(VMEM,) * 5,
        cost_estimate=WORK,
        compiler_params=PARAMS,
        name="inner_cells",
    )(*cells, *partial, *beside)

    corner = f32((4, columns))
    corners = pl.pallas_call(
        corner_kernel,
        out_shape=(corner,) * len(along_rows),
        in_specs=[VMEM] * 2 + [ANY],
        out_specs=(VMEM,) * len(along_rows),
        compiler_params=PARAMS,
        name="corner_rows",
    )(*old_far[::-1], inner[4])
    corners = [paired(value, pairs) for value, pairs in zip(corners, along_rows)]
    fed, auto, middle = pl.pallas_call(
        functools.partial(second_kernel, len(corners)),
        out_shape=(whole, whole, f32((5, rows, columns))),
        in_specs=[VMEM] * (13 + len(corners)),
        out_specs=(VMEM,) * 3,
        cost_estimate=WORK,
        compiler_params=PARAMS,
        name="second_step",
    )(*cells, extinction, mix, *inner, *old_far, *corners)

    block = columns // count
    group = packing(rows, block)
    held = pltpu.VMEM(whole.shape, jnp.float32)
    fed, auto, part = pl.pallas_call(
        functools.partial(shade_kernel, count),
        out_shape=(held, held, f32((count, 4 * rows // group, LANES) if group else (4, rows, columns))),
        in_specs=[VMEM] * 7,
        out_specs=(VMEM,) * 3,
        compiler_params=PARAMS,
        name="shading",
    )(fed, auto, extinction, mix, middle, *new_far)
    if not group:
        part = jnp.transpose(part.reshape(4 * rows, count, block), (1, 0, 2))
    part = lax.all_to_all(part, "depth", 0, 0)
    image = f32((4, rows, block))
    image, fed, auto = pl.pallas_call(
        functools.partial(last_kernel, group or 1),
        out_shape=(image, whole, whole),
        in_specs=[VMEM] * 3,
        out_specs=(HBM,) * 3,
        scratch_shapes=[pltpu.VMEM(image.shape, jnp.float32), pltpu.SemaphoreType.DMA((3,))],
        compiler_params=PARAMS,
        name="front_to_back",
    )(part, fed, auto)
    return fed, auto, image


def solution(mesh):
    cells = P("depth", "rows", None)
    return jax.shard_map(
        body,
        mesh=mesh,
        in_specs=(cells,) * 5 + (P(),),
        out_specs=(cells, cells, P(None, "rows", "depth")),
        check_vma=False,
    )
```

```python
import functools

import jax
import jax.numpy as jnp
from jax import lax
from jax.experimental import pallas as pl
from jax.experimental.pallas import tpu as pltpu
from jax.sharding import PartitionSpec as P

diffusion_fast = 0.08
diffusion_slow = 0.04
time_step = 2.0
reach_fast = time_step * diffusion_fast
reach_slow = time_step * diffusion_slow
LANES = 128
SUBLANES = 8
VMEM = pl.BlockSpec(memory_space=pltpu.VMEM)
SMEM = pl.BlockSpec(memory_space=pltpu.SMEM)
HBM = pl.BlockSpec(memory_space=pltpu.HBM)
ANY = pl.BlockSpec(memory_space=pl.ANY)
WORK = pl.CostEstimate(flops=20_000_000, bytes_accessed=4_000_000, transcendentals=0)
PARAMS = pltpu.CompilerParams(vmem_limit_bytes=24 * 1024 * 1024)


def pairings(axis, other):
    count, width = lax.axis_size(axis), lax.axis_size(other)
    flat = (lambda i, j: i * width + j) if axis == "depth" else (lambda i, j: j * count + i)
    result = []
    for shift in (0, 1):
        pairs = []
        for i in range(count):
            partner = ((i + shift) ^ 1) - shift
            for j in range(width):
                if 0 <= partner < count:
                    pairs.append((flat(i, j), flat(partner, j)))
                elif j ^ 1 < width:
                    pairs.append((flat(i, j), flat(i, j ^ 1)))
        result.append(pairs if count > 2 or shift == 0 else None)
    return result


def paired(value, pairs):
    return lax.ppermute(value, ("depth", "rows"), pairs)


def is_even(axis):
    return lax.rem(lax.axis_index(axis), 2) == 0


def shifted_columns(value):
    width = value.shape[-1]
    column = lax.broadcasted_iota(jnp.int32, value.shape, value.ndim - 1)
    left = jnp.where(column == 0, 0.0, pltpu.roll(value, 1, value.ndim - 1))
    right = jnp.where(column == width - 1, 0.0, pltpu.roll(value, width - 1, value.ndim - 1))
    return left + right


def shifted_rows(value, above, below):
    rows = value.shape[0]
    row = lax.broadcasted_iota(jnp.int32, value.shape, 0)
    upper = jnp.where(row == 0, above, pltpu.roll(value, 1, 0))
    lower = jnp.where(row == rows - 1, below, pltpu.roll(value, rows - 1, 0))
    return upper + lower


def react(fed, auto, fed_near, auto_near, feed, kill):
    reaction = fed * auto * auto
    fed_change = diffusion_fast * (fed_near - 6.0 * fed) - reaction + feed * (1.0 - fed)
    auto_change = diffusion_slow * (auto_near - 6.0 * auto) + reaction - (feed + kill) * auto
    return fed + time_step * fed_change, auto + time_step * auto_change


def partial_step(s_ref, c_ref, feed, kill, layer, inner):
    near = []
    for ref in (s_ref, c_ref):
        value = ref[layer]
        total = shifted_rows(value, 0.0, 0.0) + shifted_columns(value)
        for other in inner:
            total = total + ref[other]
        near.append(total)
    return react(s_ref[layer], c_ref[layer], near[0], near[1], feed, kill)


def old_kernel(s_hbm, c_hbm, palette_hbm, *refs):
    b_ref, a_ref, mix_ref, palette, arrived = refs[-5:]
    depth, _, columns = s_hbm.shape
    even = is_even("depth")
    copies = []
    for n, (out, towards_next) in enumerate(((a_ref, even), (b_ref, jnp.logical_not(even)))):
        layer = jnp.where(towards_next, depth - 1, 0)
        for i, hbm in enumerate((s_hbm, c_hbm)):
            copies.append(pltpu.make_async_copy(hbm.at[layer], out.at[i], arrived.at[n, i]))
    copies.append(pltpu.make_async_copy(palette_hbm, palette, arrived.at[2, 0]))
    for copy in copies:
        copy.start()
    copies[-1].wait()
    for channel in range(3):
        for n, scale in enumerate((8.0, 8.0, 1.0)):
            at = 3 * channel + n
            mix_ref[at : at + 1] = jnp.full((1, columns), scale * palette[channel, n], jnp.float32)
    for copy in copies[:-1]:
        copy.wait()


def partial_kernel(s_ref, c_ref, f_ref, k_ref, _, ps_ref, pc_ref, b_ref, a_ref, *strips):
    depth, rows, _ = s_ref.shape
    for layer in range(depth):
        inner = [other for other in (layer - 1, layer + 1) if 0 <= other < depth]
        ps_ref[layer], pc_ref[layer] = partial_step(s_ref, c_ref, f_ref[layer], k_ref[layer], layer, inner)
    even = is_even("depth")
    for out, towards_next in ((a_ref, even), (b_ref, jnp.logical_not(even))):
        layer = jnp.where(towards_next, depth - 1, 0)
        out[0] = ps_ref[layer]
        out[1] = pc_ref[layer]
    even = is_even("rows")
    for out, towards_next in zip(strips, (even, jnp.logical_not(even))):
        for n, ref in enumerate((s_ref, c_ref, ps_ref, pc_ref)):
            for layer in range(depth):
                head, tail = ref[layer, 0:1], ref[layer, rows - 1 : rows]
                out[n * depth + layer : n * depth + layer + 1] = jnp.where(towards_next, tail, head)


def sides(axis, refs, read):
    index, count = lax.axis_index(axis), lax.axis_size(axis)
    even = is_even(axis)
    first = read(refs[0])
    second = read(refs[1]) if len(refs) == 2 else 0.0
    before = jnp.where(even, second, first)
    after = jnp.where(even, first, second)
    return jnp.where(index == 0, 0.0, before), jnp.where(index == count - 1, 0.0, after)


def step_two(fields, outside, layer, others, feed, kill):
    near = []
    for n in range(2):
        value = fields[n][layer]
        total = shifted_rows(value, outside[n][layer][0], outside[n][layer][1]) + shifted_columns(value)
        for other in others[n]:
            total = total + other
        near.append(total)
    return react(fields[0][layer], fields[1][layer], near[0], near[1], feed, kill)


def inner_kernel(s_ref, c_ref, f_ref, k_ref, ps_ref, pc_ref, *refs):
    *beside, fed_one, auto_one, fed_two, auto_two, outer_ref = refs
    depth, rows, columns = s_ref.shape
    row = lax.broadcasted_iota(jnp.int32, (rows, columns), 0)
    index, last = lax.axis_index("rows"), lax.axis_size("rows") - 1
    inside = (index > 0, index < last)
    fields, outside = [], []
    for n, (old, partial, out, reach) in enumerate(
        ((s_ref, ps_ref, fed_one, reach_fast), (c_ref, pc_ref, auto_one, reach_slow))
    ):
        values, rows_outside = [], []
        for layer in range(depth):
            at = n * depth + layer
            above, below = sides("rows", beside, lambda ref: ref[at : at + 1])
            near = jnp.where(row == 0, above, 0.0) + jnp.where(row == rows - 1, below, 0.0)
            value = partial[layer] + reach * near
            values.append(value)
            out[layer] = value
            at = (2 + n) * depth + layer
            beyond = sides("rows", beside, lambda ref: ref[at : at + 1])
            ends = []
            for side, own in enumerate((old[layer, 0:1], old[layer, rows - 1 : rows])):
                end = jnp.where(inside[side], beyond[side] + reach * own, 0.0)
                ends.append(end)
                at = (n * 2 + side) * depth + layer
                outer_ref[at : at + 1] = end
            rows_outside.append(ends)
        fields.append(values)
        outside.append(rows_outside)
    for layer in range(1, depth - 1):
        others = [(values[layer - 1], values[layer + 1]) for values in fields]
        fed_two[layer], auto_two[layer] = step_two(fields, outside, layer, others, f_ref[layer], k_ref[layer])


def corner_kernel(b_ref, a_ref, _, *outs):
    rows = a_ref.shape[1]
    even = is_even("rows")
    for out, towards_next in zip(outs, (even, jnp.logical_not(even))):
        for n in range(2):
            pair = sides(
                "depth",
                (a_ref, b_ref),
                lambda ref: jnp.where(towards_next, ref[n, rows - 1 : rows], ref[n, 0:1]),
            )
            for end in range(2):
                out[2 * n + end : 2 * n + end + 1] = pair[end]


class Shading:
    def __init__(self, mix_ref):
        self.mix = [[mix_ref[3 * k + n : 3 * k + n + 1] for n in range(3)] for k in range(3)]
        self.gather = None
        self.before = None

    def put(self, pieces, passing):
        if self.gather is None:
            self.gather, self.before = list(pieces), passing
            return
        self.gather = [total + self.before * piece for total, piece in zip(self.gather, pieces)]
        self.before = self.before * passing

    def add(self, fed, auto, extinction):
        passing = jnp.exp(-extinction * (0.25 + 4.0 * auto * auto))
        opacity = 1.0 - passing
        pieces = []
        for fed_mix, auto_mix, offset in self.mix:
            level = fed_mix * (fed - 0.65) + auto_mix * (auto - 0.25) + offset
            pieces.append(opacity / (1.0 + jnp.exp(-level)))
        self.put(pieces + [opacity], passing)


def second_kernel(row_pairings, *refs):
    s_ref, c_ref, f_ref, k_ref, e_ref, mix_ref = refs[:6]
    fed_one, auto_one, fed_mid, auto_mid, outer_ref = refs[6:11]
    far = refs[11:13]
    corners = refs[13 : 13 + row_pairings]
    fed_two, auto_two, middle_ref = refs[13 + row_pairings :]
    depth, rows, columns = s_ref.shape
    row = lax.broadcasted_iota(jnp.int32, (rows, columns), 0)
    index, last = lax.axis_index("depth"), lax.axis_size("depth") - 1
    inside = (index > 0, index < last)
    ends = (0, depth - 1)
    fields, outside, beyond, far_old = [], [], [], []
    for n, (old, one, reach) in enumerate(((s_ref, fed_one, reach_fast), (c_ref, auto_one, reach_slow))):
        old_far = sides("depth", far, lambda ref: ref[n])
        far_old.append(old_far)
        beyond.append([])
        values, rows_outside = {}, {}
        for end, layer in enumerate(ends):
            at = 2 * n + end
            above, below = sides("rows", corners, lambda ref: ref[at : at + 1])
            corner = jnp.where(row == 0, above, 0.0) + jnp.where(row == rows - 1, below, 0.0)
            beyond[n].append(jnp.where(inside[end], reach * old[layer], 0.0) + (2.0 * reach) * corner)
        for layer in set(ends):
            near = 0.0
            for end in range(2):
                if layer == ends[end]:
                    near = near + old_far[end]
            values[layer] = one[layer] + reach * near
            rows_outside[layer] = [
                outer_ref[(n * 2 + side) * depth + layer : (n * 2 + side) * depth + layer + 1] for side in range(2)
            ]
        fields.append(values)
        outside.append(rows_outside)
    shading = Shading(mix_ref)
    for layer in range(depth):
        if layer in ends:
            others = []
            for n, one in enumerate((fed_one, auto_one)):
                others.append(
                    [
                        beyond[n][0] if layer == 0 else fields[n].get(layer - 1, one[layer - 1]),
                        beyond[n][1] if layer == depth - 1 else fields[n].get(layer + 1, one[layer + 1]),
                    ]
                )
            fed, auto = step_two(fields, outside, layer, others, f_ref[layer], k_ref[layer])
        else:
            fed, auto = fed_mid[layer], auto_mid[layer]
            for end, beside in enumerate((1, depth - 2)):
                if layer == beside:
                    fed = fed + (reach_fast * reach_fast) * far_old[0][end]
                    auto = auto + (reach_slow * reach_slow) * far_old[1][end]
            shading.add(fed, auto, e_ref[layer])
        fed_two[layer] = fed
        auto_two[layer] = auto
    if shading.gather is not None:
        for n, value in enumerate(shading.gather + [shading.before]):
            middle_ref[n] = value


def shade_kernel(depth_count, fed_two, auto_two, e_ref, mix_ref, middle_ref, b_ref, a_ref, fed_out, auto_out, part_ref):
    depth, rows, columns = fed_two.shape
    new_far = [sides("depth", (a_ref, b_ref), lambda ref: ref[n]) for n in range(2)]
    shading = Shading(mix_ref)
    for layer in range(depth):
        fed, auto = fed_two[layer], auto_two[layer]
        if layer in (0, depth - 1):
            for end, place in enumerate((0, depth - 1)):
                if layer == place:
                    fed = fed + reach_fast * new_far[0][end]
                    auto = auto + reach_slow * new_far[1][end]
            shading.add(fed, auto, e_ref[layer])
        elif layer == 1:
            shading.put([middle_ref[n] for n in range(4)], middle_ref[4])
        fed_out[layer] = fed
        auto_out[layer] = auto
    gather = shading.gather

    block = columns // depth_count
    group = packing(rows, block)
    if not group:
        for channel in range(4):
            part_ref[channel] = gather[channel]
        return
    high = rows // group
    lane = lax.broadcasted_iota(jnp.int32, (high, LANES), 1) // block
    for channel in range(4):
        for tile in range(columns // LANES):
            pieces = [
                gather[channel][q * high : (q + 1) * high, tile * LANES : (tile + 1) * LANES]
                for q in range(group)
            ]
            for p in range(group):
                packed = None
                for q in range(group):
                    turn = (q - p) * block % LANES
                    piece = pltpu.roll(pieces[q], turn, 1) if turn else pieces[q]
                    packed = piece if packed is None else jnp.where(lane == q, piece, packed)
                part_ref[tile * group + p, channel * high : (channel + 1) * high] = packed


def packing(rows, block):
    if block >= LANES or LANES % block:
        return 0
    group = LANES // block
    return group if rows % (group * SUBLANES) == 0 else 0


def last_kernel(group, part_ref, fed_ref, auto_ref, image_out, fed_out, auto_out, image_ref, written):
    copies = [
        pltpu.make_async_copy(ref, out, written.at[n])
        for n, (ref, out) in enumerate(((fed_ref, fed_out), (auto_ref, auto_out), (image_ref, image_out)))
    ]
    copies[0].start()
    copies[1].start()
    _, rows, block = image_ref.shape
    high = rows // group
    count = part_ref.shape[0]
    total = [part_ref[0, channel * high : (channel + 1) * high] for channel in range(4)]
    before = 1.0 - total[3]
    for n in range(1, count):
        for channel in range(4):
            piece = part_ref[n, channel * high : (channel + 1) * high]
            total[channel] = total[channel] + before * piece
        if n < count - 1:
            before = before * (1.0 - piece)
    for channel in range(4):
        for q in range(group):
            image_ref[channel, q * high : (q + 1) * high] = total[channel][:, q * block : (q + 1) * block]
    copies[2].start()
    for copy in copies:
        copy.wait()


def body(substrate, catalyst, feed_rate, kill_rate, extinction, palette):
    depth, rows, columns = substrate.shape
    count = lax.axis_size("depth")
    f32 = functools.partial(jax.ShapeDtypeStruct, dtype=jnp.float32)
    whole = f32(substrate.shape)
    along_depth = pairings("depth", "rows")
    if along_depth[1] is None:
        along_depth[1] = along_depth[0]
    along_rows = [pairs for pairs in pairings("rows", "depth") if pairs is not None]

    cells = (substrate, catalyst, feed_rate, kill_rate)
    pair = f32((2, rows, columns))
    in_hbm = lambda x: pltpu.with_memory_space_constraint(x, pltpu.HBM)
    *old_beams, mix = pl.pallas_call(
        old_kernel,
        out_shape=(pair, pair, f32((9, columns))),
        in_specs=[HBM] * 6,
        out_specs=(VMEM,) * 3,
        scratch_shapes=[pltpu.SMEM(palette.shape, jnp.float32), pltpu.SemaphoreType.DMA((3, 2))],
        cost_estimate=WORK,
        compiler_params=PARAMS,
        name="old_layers",
    )(*(in_hbm(x) for x in (substrate, catalyst, palette, feed_rate, kill_rate, extinction)))
    old_far = [paired(value, pairs) for value, pairs in zip(old_beams[::-1], along_depth)]

    strip = f32((4 * depth, columns))
    outs = pl.pallas_call(
        partial_kernel,
        out_shape=(whole, whole, pair, pair) + (strip,) * len(along_rows),
        in_specs=[VMEM] * 4 + [ANY],
        out_specs=(VMEM,) * (4 + len(along_rows)),
        cost_estimate=WORK,
        compiler_params=PARAMS,
        name="partial_step",
    )(*cells, old_beams[0])
    partial = outs[:2]
    new_far = [paired(value, pairs) for value, pairs in zip((outs[3], outs[2]), along_depth)]
    beside = [paired(value, pairs) for value, pairs in zip(outs[4:], along_rows)]
    inner = pl.pallas_call(
        inner_kernel,
        out_shape=(whole,) * 4 + (strip,),
        in_specs=[VMEM] * (6 + len(beside)),
        out_specs=(VMEM,) * 5,
        cost_estimate=WORK,
        compiler_params=PARAMS,
        name="inner_cells",
    )(*cells, *partial, *beside)

    corner = f32((4, columns))
    corners = pl.pallas_call(
        corner_kernel,
        out_shape=(corner,) * len(along_rows),
        in_specs=[VMEM] * 2 + [ANY],
        out_specs=(VMEM,) * len(along_rows),
        compiler_params=PARAMS,
        name="corner_rows",
    )(*old_far[::-1], inner[4])
    corners = [paired(value, pairs) for value, pairs in zip(corners, along_rows)]
    fed, auto, middle = pl.pallas_call(
        functools.partial(second_kernel, len(corners)),
        out_shape=(whole, whole, f32((5, rows, columns))),
        in_specs=[VMEM] * (13 + len(corners)),
        out_specs=(VMEM,) * 3,
        cost_estimate=WORK,
        compiler_params=PARAMS,
        name="second_step",
    )(*cells, extinction, mix, *inner, *old_far, *corners)

    block = columns // count
    group = packing(rows, block)
    held = pltpu.VMEM(whole.shape, jnp.float32)
    fed, auto, part = pl.pallas_call(
        functools.partial(shade_kernel, count),
        out_shape=(held, held, f32((count, 4 * rows // group, LANES) if group else (4, rows, columns))),
        in_specs=[VMEM] * 7,
        out_specs=(VMEM,) * 3,
        compiler_params=PARAMS,
        name="shading",
    )(fed, auto, extinction, mix, middle, *new_far[::-1])
    if not group:
        part = jnp.transpose(part.reshape(4 * rows, count, block), (1, 0, 2))
    part = lax.all_to_all(part, "depth", 0, 0)
    image = f32((4, rows, block))
    image, fed, auto = pl.pallas_call(
        functools.partial(last_kernel, group or 1),
        out_shape=(image, whole, whole),
        in_specs=[VMEM] * 3,
        out_specs=(HBM,) * 3,
        scratch_shapes=[pltpu.VMEM(image.shape, jnp.float32), pltpu.SemaphoreType.DMA((3,))],
        compiler_params=PARAMS,
        name="front_to_back",
    )(part, fed, auto)
    return fed, auto, image


def solution(mesh):
    cells = P("depth", "rows", None)
    return jax.shard_map(
        body,
        mesh=mesh,
        in_specs=(cells,) * 5 + (P(),),
        out_specs=(cells, cells, P(None, "rows", "depth")),
        check_vma=False,
    )
```

```python
import functools

import jax
import jax.numpy as jnp
from jax import lax
from jax.experimental import pallas as pl
from jax.experimental.pallas import tpu as pltpu
from jax.sharding import PartitionSpec as P

diffusion_fast = 0.08
diffusion_slow = 0.04
time_step = 2.0
reach_fast = time_step * diffusion_fast
reach_slow = time_step * diffusion_slow
LANES = 128
SUBLANES = 8
VMEM = pl.BlockSpec(memory_space=pltpu.VMEM)
SMEM = pl.BlockSpec(memory_space=pltpu.SMEM)
HBM = pl.BlockSpec(memory_space=pltpu.HBM)
ANY = pl.BlockSpec(memory_space=pl.ANY)
WORK = pl.CostEstimate(flops=20_000_000, bytes_accessed=4_000_000, transcendentals=0)
PARAMS = pltpu.CompilerParams(vmem_limit_bytes=24 * 1024 * 1024)


def pairings(axis, other):
    count, width = lax.axis_size(axis), lax.axis_size(other)
    flat = (lambda i, j: i * width + j) if axis == "depth" else (lambda i, j: j * count + i)
    result = []
    for shift in (0, 1):
        pairs = []
        for i in range(count):
            partner = ((i + shift) ^ 1) - shift
            for j in range(width):
                if 0 <= partner < count:
                    pairs.append((flat(i, j), flat(partner, j)))
                elif j ^ 1 < width:
                    pairs.append((flat(i, j), flat(i, j ^ 1)))
        result.append(pairs if count > 2 or shift == 0 else None)
    return result


def paired(value, pairs):
    return lax.ppermute(value, ("depth", "rows"), pairs)


def is_even(axis):
    return lax.rem(lax.axis_index(axis), 2) == 0


def partners(axis):
    index, last = lax.axis_index(axis), lax.axis_size(axis) - 1
    odd = lax.rem(index, 2)
    return [jnp.clip(index + 1 - 2 * odd, 0, last), jnp.clip(index - 1 + 2 * odd, 0, last)]


def shifted_columns(value):
    width = value.shape[-1]
    column = lax.broadcasted_iota(jnp.int32, value.shape, value.ndim - 1)
    left = jnp.where(column == 0, 0.0, pltpu.roll(value, 1, value.ndim - 1))
    right = jnp.where(column == width - 1, 0.0, pltpu.roll(value, width - 1, value.ndim - 1))
    return left + right


def shifted_rows(value, above, below):
    rows = value.shape[0]
    row = lax.broadcasted_iota(jnp.int32, value.shape, 0)
    upper = jnp.where(row == 0, above, pltpu.roll(value, 1, 0))
    lower = jnp.where(row == rows - 1, below, pltpu.roll(value, rows - 1, 0))
    return upper + lower


def react(fed, auto, fed_near, auto_near, feed, kill):
    reaction = fed * auto * auto
    fed_change = diffusion_fast * (fed_near - 6.0 * fed) - reaction + feed * (1.0 - fed)
    auto_change = diffusion_slow * (auto_near - 6.0 * auto) + reaction - (feed + kill) * auto
    return fed + time_step * fed_change, auto + time_step * auto_change


def partial_step(s_ref, c_ref, feed, kill, layer, inner):
    near = []
    for ref in (s_ref, c_ref):
        value = ref[layer]
        total = shifted_rows(value, 0.0, 0.0) + shifted_columns(value)
        for other in inner:
            total = total + ref[other]
        near.append(total)
    return react(s_ref[layer], c_ref[layer], near[0], near[1], feed, kill)


def old_kernel(s_hbm, c_hbm, palette_hbm, *refs):
    b_ref, a_ref, mix_ref, palette, arrived = refs[-5:]
    depth, _, columns = s_hbm.shape
    even = is_even("depth")
    copies = []
    for n, (out, towards_next) in enumerate(((a_ref, even), (b_ref, jnp.logical_not(even)))):
        layer = jnp.where(towards_next, depth - 1, 0)
        for i, hbm in enumerate((s_hbm, c_hbm)):
            copies.append(pltpu.make_async_copy(hbm.at[layer], out.at[i], arrived.at[n, i]))
    copies.append(pltpu.make_async_copy(palette_hbm, palette, arrived.at[2, 0]))
    for copy in copies:
        copy.start()
    copies[-1].wait()
    for channel in range(3):
        for n, scale in enumerate((8.0, 8.0, 1.0)):
            at = 3 * channel + n
            mix_ref[at : at + 1] = jnp.full((1, columns), scale * palette[channel, n], jnp.float32)
    for copy in copies[:-1]:
        copy.wait()


def partial_kernel(s_ref, c_ref, f_ref, k_ref, _, ps_ref, pc_ref, a_ref, *strips):
    depth, rows, _ = s_ref.shape
    for layer in range(depth):
        inner = [other for other in (layer - 1, layer + 1) if 0 <= other < depth]
        ps_ref[layer], pc_ref[layer] = partial_step(s_ref, c_ref, f_ref[layer], k_ref[layer], layer, inner)
    layer = jnp.where(is_even("depth"), depth - 1, 0)
    a_ref[0] = ps_ref[layer]
    a_ref[1] = pc_ref[layer]
    even = is_even("rows")
    for out, towards_next in zip(strips, (even, jnp.logical_not(even))):
        for n, ref in enumerate((s_ref, c_ref, ps_ref, pc_ref)):
            for layer in range(depth):
                head, tail = ref[layer, 0:1], ref[layer, rows - 1 : rows]
                out[n * depth + layer : n * depth + layer + 1] = jnp.where(towards_next, tail, head)


def sides(axis, refs, read):
    index, count = lax.axis_index(axis), lax.axis_size(axis)
    even = is_even(axis)
    first = read(refs[0])
    second = read(refs[1]) if len(refs) == 2 else 0.0
    before = jnp.where(even, second, first)
    after = jnp.where(even, first, second)
    return jnp.where(index == 0, 0.0, before), jnp.where(index == count - 1, 0.0, after)


def step_two(fields, outside, layer, others, feed, kill):
    near = []
    for n in range(2):
        value = fields[n][layer]
        total = shifted_rows(value, outside[n][layer][0], outside[n][layer][1]) + shifted_columns(value)
        for other in others[n]:
            total = total + other
        near.append(total)
    return react(fields[0][layer], fields[1][layer], near[0], near[1], feed, kill)


def inner_kernel(s_ref, c_ref, f_ref, k_ref, ps_ref, pc_ref, *refs):
    *strips, fed_one, auto_one, fed_two, auto_two, outer_ref, b_ref = refs
    beside = [ref.at[place] for ref, place in zip(strips, partners("rows"))]
    depth, rows, columns = s_ref.shape
    row = lax.broadcasted_iota(jnp.int32, (rows, columns), 0)
    index, last = lax.axis_index("rows"), lax.axis_size("rows") - 1
    inside = (index > 0, index < last)
    fields, outside = [], []
    for n, (old, partial, out, reach) in enumerate(
        ((s_ref, ps_ref, fed_one, reach_fast), (c_ref, pc_ref, auto_one, reach_slow))
    ):
        values, rows_outside = [], []
        for layer in range(depth):
            at = n * depth + layer
            above, below = sides("rows", beside, lambda ref: ref[at : at + 1])
            near = jnp.where(row == 0, above, 0.0) + jnp.where(row == rows - 1, below, 0.0)
            value = partial[layer] + reach * near
            values.append(value)
            out[layer] = value
            at = (2 + n) * depth + layer
            beyond = sides("rows", beside, lambda ref: ref[at : at + 1])
            ends = []
            for side, own in enumerate((old[layer, 0:1], old[layer, rows - 1 : rows])):
                end = jnp.where(inside[side], beyond[side] + reach * own, 0.0)
                ends.append(end)
                at = (n * 2 + side) * depth + layer
                outer_ref[at : at + 1] = end
            rows_outside.append(ends)
        fields.append(values)
        outside.append(rows_outside)
    for layer in range(1, depth - 1):
        others = [(values[layer - 1], values[layer + 1]) for values in fields]
        fed_two[layer], auto_two[layer] = step_two(fields, outside, layer, others, f_ref[layer], k_ref[layer])
    end = jnp.where(is_even("depth"), 0, depth - 1)
    for n, (one, partial) in enumerate(((fed_one, ps_ref), (auto_one, pc_ref))):
        b_ref[n] = one[end] + (one[end] - partial[end])


def corner_kernel(depth, *refs):
    *strips, out = refs
    beside = [ref.at[place] for ref, place in zip(strips, partners("rows"))]
    even = is_even("depth")
    for n in range(2):
        first, final = [
            sides("rows", beside, lambda ref: ref[n * depth + layer : n * depth + layer + 1])
            for layer in (0, depth - 1)
        ]
        for side in range(2):
            out[2 * n + side : 2 * n + side + 1] = jnp.where(even, final[side], first[side])


class Shading:
    def __init__(self, mix_ref):
        self.mix = [[mix_ref[3 * k + n : 3 * k + n + 1] for n in range(3)] for k in range(3)]
        self.gather = None
        self.before = None

    def put(self, pieces, passing):
        if self.gather is None:
            self.gather, self.before = list(pieces), passing
            return
        self.gather = [total + self.before * piece for total, piece in zip(self.gather, pieces)]
        self.before = self.before * passing

    def add(self, fed, auto, extinction):
        passing = jnp.exp(-extinction * (0.25 + 4.0 * auto * auto))
        opacity = 1.0 - passing
        pieces = []
        for fed_mix, auto_mix, offset in self.mix:
            level = fed_mix * (fed - 0.65) + auto_mix * (auto - 0.25) + offset
            pieces.append(opacity / (1.0 + jnp.exp(-level)))
        self.put(pieces + [opacity], passing)


def second_kernel(*refs):
    s_ref, c_ref, f_ref, k_ref, e_ref, mix_ref = refs[:6]
    fed_one, auto_one, fed_mid, auto_mid, outer_ref = refs[6:11]
    far = refs[11:13]
    fed_two, auto_two, middle_ref = refs[13:]
    depth = s_ref.shape[0]
    index, last = lax.axis_index("depth"), lax.axis_size("depth") - 1
    inside = (index > 0, index < last)
    ends = (0, depth - 1)
    fields, outside, beyond, far_old = [], [], [], []
    for n, (old, one, reach) in enumerate(((s_ref, fed_one, reach_fast), (c_ref, auto_one, reach_slow))):
        old_far = sides("depth", far, lambda ref: ref[n])
        far_old.append(old_far)
        beyond.append([])
        values, rows_outside = {}, {}
        for end, layer in enumerate(ends):
            beyond[n].append(jnp.where(inside[end], reach * old[layer], 0.0))
        for layer in set(ends):
            near = 0.0
            for end in range(2):
                if layer == ends[end]:
                    near = near + old_far[end]
            values[layer] = one[layer] + reach * near
            rows_outside[layer] = [
                outer_ref[(n * 2 + side) * depth + layer : (n * 2 + side) * depth + layer + 1] for side in range(2)
            ]
        fields.append(values)
        outside.append(rows_outside)
    shading = Shading(mix_ref)
    for layer in range(depth):
        if layer in ends:
            others = []
            for n, one in enumerate((fed_one, auto_one)):
                others.append(
                    [
                        beyond[n][0] if layer == 0 else fields[n].get(layer - 1, one[layer - 1]),
                        beyond[n][1] if layer == depth - 1 else fields[n].get(layer + 1, one[layer + 1]),
                    ]
                )
            fed, auto = step_two(fields, outside, layer, others, f_ref[layer], k_ref[layer])
        else:
            fed, auto = fed_mid[layer], auto_mid[layer]
            for end, beside in enumerate((1, depth - 2)):
                if layer == beside:
                    fed = fed + (reach_fast * reach_fast) * far_old[0][end]
                    auto = auto + (reach_slow * reach_slow) * far_old[1][end]
            shading.add(fed, auto, e_ref[layer])
        fed_two[layer] = fed
        auto_two[layer] = auto
    if shading.gather is not None:
        for n, value in enumerate(shading.gather + [shading.before]):
            middle_ref[n] = value


def shade_kernel(depth_count, *refs):
    fed_two, auto_two, e_ref, mix_ref, middle_ref, a_ref, b_ref, corner_ref, fed_out, auto_out, part_ref = refs
    depth, rows, columns = fed_two.shape
    row = lax.broadcasted_iota(jnp.int32, (rows, columns), 0)
    index = lax.axis_index("depth")
    even = is_even("depth")
    there = (
        jnp.logical_and(jnp.logical_not(even), index > 0),
        jnp.logical_and(even, index < depth_count - 1),
    )
    more = []
    for n, reach in enumerate((reach_fast, reach_slow)):
        new_far = sides("depth", (a_ref, b_ref), lambda ref: ref[n])
        above, below = corner_ref[2 * n : 2 * n + 1], corner_ref[2 * n + 1 : 2 * n + 2]
        corner = jnp.where(row == 0, above, 0.0) + jnp.where(row == rows - 1, below, 0.0)
        more.append(
            [reach * new_far[end] + jnp.where(there[end], (2.0 * reach * reach) * corner, 0.0) for end in range(2)]
        )
    shading = Shading(mix_ref)
    for layer in range(depth):
        fed, auto = fed_two[layer], auto_two[layer]
        if layer in (0, depth - 1):
            for end, place in enumerate((0, depth - 1)):
                if layer == place:
                    fed = fed + more[0][end]
                    auto = auto + more[1][end]
            shading.add(fed, auto, e_ref[layer])
        elif layer == 1:
            shading.put([middle_ref[n] for n in range(4)], middle_ref[4])
        fed_out[layer] = fed
        auto_out[layer] = auto
    gather = shading.gather

    block = columns // depth_count
    group = packing(rows, block)
    if not group:
        for channel in range(4):
            part_ref[channel] = gather[channel]
        return
    high = rows // group
    lane = lax.broadcasted_iota(jnp.int32, (high, LANES), 1) // block
    for channel in range(4):
        for tile in range(columns // LANES):
            pieces = [
                gather[channel][q * high : (q + 1) * high, tile * LANES : (tile + 1) * LANES]
                for q in range(group)
            ]
            for p in range(group):
                packed = None
                for q in range(group):
                    turn = (q - p) * block % LANES
                    piece = pltpu.roll(pieces[q], turn, 1) if turn else pieces[q]
                    packed = piece if packed is None else jnp.where(lane == q, piece, packed)
                part_ref[tile * group + p, channel * high : (channel + 1) * high] = packed


def packing(rows, block):
    if block >= LANES or LANES % block:
        return 0
    group = LANES // block
    return group if rows % (group * SUBLANES) == 0 else 0


def last_kernel(group, part_ref, fed_ref, auto_ref, image_out, fed_out, auto_out, image_ref, written):
    copies = [
        pltpu.make_async_copy(ref, out, written.at[n])
        for n, (ref, out) in enumerate(((fed_ref, fed_out), (auto_ref, auto_out), (image_ref, image_out)))
    ]
    copies[0].start()
    copies[1].start()
    _, rows, block = image_ref.shape
    high = rows // group
    count = part_ref.shape[0]
    total = [part_ref[0, channel * high : (channel + 1) * high] for channel in range(4)]
    before = 1.0 - total[3]
    for n in range(1, count):
        for channel in range(4):
            piece = part_ref[n, channel * high : (channel + 1) * high]
            total[channel] = total[channel] + before * piece
        if n < count - 1:
            before = before * (1.0 - piece)
    for channel in range(4):
        for q in range(group):
            image_ref[channel, q * high : (q + 1) * high] = total[channel][:, q * block : (q + 1) * block]
    copies[2].start()
    for copy in copies:
        copy.wait()


def body(substrate, catalyst, feed_rate, kill_rate, extinction, palette):
    depth, rows, columns = substrate.shape
    count = lax.axis_size("depth")
    f32 = functools.partial(jax.ShapeDtypeStruct, dtype=jnp.float32)
    whole = f32(substrate.shape)
    along_depth = pairings("depth", "rows")
    if along_depth[1] is None:
        along_depth[1] = along_depth[0]
    along_rows = [pairs for pairs in pairings("rows", "depth") if pairs is not None]

    cells = (substrate, catalyst, feed_rate, kill_rate)
    pair = f32((2, rows, columns))
    in_hbm = lambda x: pltpu.with_memory_space_constraint(x, pltpu.HBM)
    *old_beams, mix = pl.pallas_call(
        old_kernel,
        out_shape=(pair, pair, f32((9, columns))),
        in_specs=[HBM] * 6,
        out_specs=(VMEM,) * 3,
        scratch_shapes=[pltpu.SMEM(palette.shape, jnp.float32), pltpu.SemaphoreType.DMA((3, 2))],
        cost_estimate=WORK,
        compiler_params=PARAMS,
        name="old_layers",
    )(*(in_hbm(x) for x in (substrate, catalyst, palette, feed_rate, kill_rate, extinction)))
    old_far = [paired(value, pairs) for value, pairs in zip(old_beams[::-1], along_depth)]

    strip = f32((4 * depth, columns))
    outs = pl.pallas_call(
        partial_kernel,
        out_shape=(whole, whole, pair) + (strip,) * len(along_rows),
        in_specs=[VMEM] * 4 + [ANY],
        out_specs=(VMEM,) * (3 + len(along_rows)),
        compiler_params=PARAMS,
        name="partial_step",
    )(*cells, old_beams[0])
    partial = outs[:2]
    new_a = paired(outs[2], along_depth[0])
    beside = [lax.all_gather(value, "rows") for value in outs[3:]]
    *inner, new_b = pl.pallas_call(
        inner_kernel,
        out_shape=(whole,) * 4 + (strip, pair),
        in_specs=[VMEM] * (6 + len(beside)),
        out_specs=(VMEM,) * 6,
        compiler_params=PARAMS,
        name="inner_cells",
    )(*cells, *partial, *beside)
    new_far = [new_a, paired(new_b, along_depth[1])]

    corner = pl.pallas_call(
        functools.partial(corner_kernel, depth),
        out_shape=f32((4, columns)),
        in_specs=[VMEM] * len(beside),
        out_specs=VMEM,
        compiler_params=PARAMS,
        name="corner_rows",
    )(*beside)
    corner = paired(corner, along_depth[0])
    fed, auto, middle = pl.pallas_call(
        second_kernel,
        out_shape=(whole, whole, f32((5, rows, columns))),
        in_specs=[VMEM] * 13,
        out_specs=(VMEM,) * 3,
        cost_estimate=WORK,
        compiler_params=PARAMS,
        name="second_step",
    )(*cells, extinction, mix, *inner, *old_far)

    block = columns // count
    group = packing(rows, block)
    held = pltpu.VMEM(whole.shape, jnp.float32)
    fed, auto, part = pl.pallas_call(
        functools.partial(shade_kernel, count),
        out_shape=(held, held, f32((count, 4 * rows // group, LANES) if group else (4, rows, columns))),
        in_specs=[VMEM] * 8,
        out_specs=(VMEM,) * 3,
        compiler_params=PARAMS,
        name="shading",
    )(fed, auto, extinction, mix, middle, *new_far, corner)
    if not group:
        part = jnp.transpose(part.reshape(4 * rows, count, block), (1, 0, 2))
    part = lax.all_to_all(part, "depth", 0, 0)
    image = f32((4, rows, block))
    image, fed, auto = pl.pallas_call(
        functools.partial(last_kernel, group or 1),
        out_shape=(image, whole, whole),
        in_specs=[VMEM] * 3,
        out_specs=(HBM,) * 3,
        scratch_shapes=[pltpu.VMEM(image.shape, jnp.float32), pltpu.SemaphoreType.DMA((3,))],
        compiler_params=PARAMS,
        name="front_to_back",
    )(part, fed, auto)
    return fed, auto, image


def solution(mesh):
    cells = P("depth", "rows", None)
    return jax.shard_map(
        body,
        mesh=mesh,
        in_specs=(cells,) * 5 + (P(),),
        out_specs=(cells, cells, P(None, "rows", "depth")),
        check_vma=False,
    )
```

```python
import functools

import jax
import jax.numpy as jnp
from jax import lax
from jax.experimental import pallas as pl
from jax.experimental.pallas import tpu as pltpu
from jax.sharding import PartitionSpec as P

diffusion_fast = 0.08
diffusion_slow = 0.04
time_step = 2.0
reach_fast = time_step * diffusion_fast
reach_slow = time_step * diffusion_slow
LANES = 128
SUBLANES = 8
VMEM = pl.BlockSpec(memory_space=pltpu.VMEM)
SMEM = pl.BlockSpec(memory_space=pltpu.SMEM)
HBM = pl.BlockSpec(memory_space=pltpu.HBM)
ANY = pl.BlockSpec(memory_space=pl.ANY)
WORK = pl.CostEstimate(flops=20_000_000, bytes_accessed=4_000_000, transcendentals=0)
PARAMS = pltpu.CompilerParams(vmem_limit_bytes=24 * 1024 * 1024)


def pairings(axis, other):
    count, width = lax.axis_size(axis), lax.axis_size(other)
    flat = (lambda i, j: i * width + j) if axis == "depth" else (lambda i, j: j * count + i)
    result = []
    for shift in (0, 1):
        pairs = []
        for i in range(count):
            partner = ((i + shift) ^ 1) - shift
            for j in range(width):
                if 0 <= partner < count:
                    pairs.append((flat(i, j), flat(partner, j)))
                elif j ^ 1 < width:
                    pairs.append((flat(i, j), flat(i, j ^ 1)))
        result.append(pairs if count > 2 or shift == 0 else None)
    return result


def paired(value, pairs):
    return lax.ppermute(value, ("depth", "rows"), pairs)


def is_even(axis):
    return lax.rem(lax.axis_index(axis), 2) == 0


def partners(axis):
    index, last = lax.axis_index(axis), lax.axis_size(axis) - 1
    odd = lax.rem(index, 2)
    return [jnp.clip(index + 1 - 2 * odd, 0, last), jnp.clip(index - 1 + 2 * odd, 0, last)]


def shifted_columns(value):
    width = value.shape[-1]
    column = lax.broadcasted_iota(jnp.int32, value.shape, value.ndim - 1)
    left = jnp.where(column == 0, 0.0, pltpu.roll(value, 1, value.ndim - 1))
    right = jnp.where(column == width - 1, 0.0, pltpu.roll(value, width - 1, value.ndim - 1))
    return left + right


def shifted_rows(value, above, below):
    rows = value.shape[0]
    row = lax.broadcasted_iota(jnp.int32, value.shape, 0)
    upper = jnp.where(row == 0, above, pltpu.roll(value, 1, 0))
    lower = jnp.where(row == rows - 1, below, pltpu.roll(value, rows - 1, 0))
    return upper + lower


def react(fed, auto, fed_near, auto_near, feed, kill):
    reaction = fed * auto * auto
    fed_change = diffusion_fast * (fed_near - 6.0 * fed) - reaction + feed * (1.0 - fed)
    auto_change = diffusion_slow * (auto_near - 6.0 * auto) + reaction - (feed + kill) * auto
    return fed + time_step * fed_change, auto + time_step * auto_change


def partial_step(s_ref, c_ref, feed, kill, layer, inner):
    near = []
    for ref in (s_ref, c_ref):
        value = ref[layer]
        total = shifted_rows(value, 0.0, 0.0) + shifted_columns(value)
        for other in inner:
            total = total + ref[other]
        near.append(total)
    return react(s_ref[layer], c_ref[layer], near[0], near[1], feed, kill)


def old_kernel(s_hbm, c_hbm, *refs):
    b_ref, a_ref, arrived = refs[-3:]
    depth = s_hbm.shape[0]
    even = is_even("depth")
    copies = []
    for n, (out, towards_next) in enumerate(((a_ref, even), (b_ref, jnp.logical_not(even)))):
        layer = jnp.where(towards_next, depth - 1, 0)
        for i, hbm in enumerate((s_hbm, c_hbm)):
            copies.append(pltpu.make_async_copy(hbm.at[layer], out.at[i], arrived.at[n, i]))
    for copy in copies:
        copy.start()
    for copy in copies:
        copy.wait()


def partial_kernel(s_ref, c_ref, f_ref, k_ref, _, ps_ref, pc_ref, a_ref, *strips):
    depth, rows, _ = s_ref.shape
    for layer in range(depth):
        inner = [other for other in (layer - 1, layer + 1) if 0 <= other < depth]
        ps_ref[layer], pc_ref[layer] = partial_step(s_ref, c_ref, f_ref[layer], k_ref[layer], layer, inner)
    layer = jnp.where(is_even("depth"), depth - 1, 0)
    a_ref[0] = ps_ref[layer]
    a_ref[1] = pc_ref[layer]
    even = is_even("rows")
    for out, towards_next in zip(strips, (even, jnp.logical_not(even))):
        for n, ref in enumerate((s_ref, c_ref, ps_ref, pc_ref)):
            for layer in range(depth):
                head, tail = ref[layer, 0:1], ref[layer, rows - 1 : rows]
                out[n * depth + layer : n * depth + layer + 1] = jnp.where(towards_next, tail, head)


def sides(axis, refs, read):
    index, count = lax.axis_index(axis), lax.axis_size(axis)
    even = is_even(axis)
    first = read(refs[0])
    second = read(refs[1]) if len(refs) == 2 else 0.0
    before = jnp.where(even, second, first)
    after = jnp.where(even, first, second)
    return jnp.where(index == 0, 0.0, before), jnp.where(index == count - 1, 0.0, after)


def step_two(fields, outside, layer, others, feed, kill):
    near = []
    for n in range(2):
        value = fields[n][layer]
        total = shifted_rows(value, outside[n][layer][0], outside[n][layer][1]) + shifted_columns(value)
        for other in others[n]:
            total = total + other
        near.append(total)
    return react(fields[0][layer], fields[1][layer], near[0], near[1], feed, kill)


def inner_kernel(s_ref, c_ref, f_ref, k_ref, ps_ref, pc_ref, *refs):
    *strips, fed_one, auto_one, fed_two, auto_two, outer_ref, b_ref = refs
    beside = [ref.at[place] for ref, place in zip(strips, partners("rows"))]
    depth, rows, columns = s_ref.shape
    row = lax.broadcasted_iota(jnp.int32, (rows, columns), 0)
    index, last = lax.axis_index("rows"), lax.axis_size("rows") - 1
    inside = (index > 0, index < last)
    fields, outside = [], []
    for n, (old, partial, out, reach) in enumerate(
        ((s_ref, ps_ref, fed_one, reach_fast), (c_ref, pc_ref, auto_one, reach_slow))
    ):
        values, rows_outside = [], []
        for layer in range(depth):
            at = n * depth + layer
            above, below = sides("rows", beside, lambda ref: ref[at : at + 1])
            near = jnp.where(row == 0, above, 0.0) + jnp.where(row == rows - 1, below, 0.0)
            value = partial[layer] + reach * near
            values.append(value)
            out[layer] = value
            at = (2 + n) * depth + layer
            beyond = sides("rows", beside, lambda ref: ref[at : at + 1])
            ends = []
            for side, own in enumerate((old[layer, 0:1], old[layer, rows - 1 : rows])):
                end = jnp.where(inside[side], beyond[side] + reach * own, 0.0)
                ends.append(end)
                at = (n * 2 + side) * depth + layer
                outer_ref[at : at + 1] = end
            rows_outside.append(ends)
        fields.append(values)
        outside.append(rows_outside)
    for layer in range(1, depth - 1):
        others = [(values[layer - 1], values[layer + 1]) for values in fields]
        fed_two[layer], auto_two[layer] = step_two(fields, outside, layer, others, f_ref[layer], k_ref[layer])
    end = jnp.where(is_even("depth"), 0, depth - 1)
    for n, (one, partial) in enumerate(((fed_one, ps_ref), (auto_one, pc_ref))):
        b_ref[n] = one[end] + (one[end] - partial[end])


def corner_kernel(depth, *refs):
    *strips, out = refs
    beside = [ref.at[place] for ref, place in zip(strips, partners("rows"))]
    even = is_even("depth")
    for n in range(2):
        first, final = [
            sides("rows", beside, lambda ref: ref[n * depth + layer : n * depth + layer + 1])
            for layer in (0, depth - 1)
        ]
        for side in range(2):
            out[2 * n + side : 2 * n + side + 1] = jnp.where(even, final[side], first[side])


class Shading:
    def __init__(self, mix_ref):
        self.mix = [[mix_ref[3 * k + n : 3 * k + n + 1] for n in range(3)] for k in range(3)]
        self.gather = None
        self.before = None

    def put(self, pieces, passing):
        if self.gather is None:
            self.gather, self.before = list(pieces), passing
            return
        self.gather = [total + self.before * piece for total, piece in zip(self.gather, pieces)]
        self.before = self.before * passing

    def add(self, fed, auto, extinction):
        passing = jnp.exp(-extinction * (0.25 + 4.0 * auto * auto))
        opacity = 1.0 - passing
        pieces = []
        for fed_mix, auto_mix, offset in self.mix:
            level = fed_mix * (fed - 0.65) + auto_mix * (auto - 0.25) + offset
            pieces.append(opacity / (1.0 + jnp.exp(-level)))
        self.put(pieces + [opacity], passing)


def second_kernel(*refs):
    s_ref, c_ref, f_ref, k_ref, e_ref, palette = refs[:6]
    fed_one, auto_one, fed_mid, auto_mid, outer_ref = refs[6:11]
    far = refs[11:13]
    fed_two, auto_two, middle_ref, mix_ref = refs[13:]
    for channel in range(3):
        for n, scale in enumerate((8.0, 8.0, 1.0)):
            at = 3 * channel + n
            mix_ref[at : at + 1] = jnp.full((1, s_ref.shape[2]), scale * palette[channel, n], jnp.float32)
    depth = s_ref.shape[0]
    index, last = lax.axis_index("depth"), lax.axis_size("depth") - 1
    inside = (index > 0, index < last)
    ends = (0, depth - 1)
    fields, outside, beyond, far_old = [], [], [], []
    for n, (old, one, reach) in enumerate(((s_ref, fed_one, reach_fast), (c_ref, auto_one, reach_slow))):
        old_far = sides("depth", far, lambda ref: ref[n])
        far_old.append(old_far)
        beyond.append([])
        values, rows_outside = {}, {}
        for end, layer in enumerate(ends):
            beyond[n].append(jnp.where(inside[end], reach * old[layer], 0.0))
        for layer in set(ends):
            near = 0.0
            for end in range(2):
                if layer == ends[end]:
                    near = near + old_far[end]
            values[layer] = one[layer] + reach * near
            rows_outside[layer] = [
                outer_ref[(n * 2 + side) * depth + layer : (n * 2 + side) * depth + layer + 1] for side in range(2)
            ]
        fields.append(values)
        outside.append(rows_outside)
    shading = Shading(mix_ref)
    for layer in range(depth):
        if layer in ends:
            others = []
            for n, one in enumerate((fed_one, auto_one)):
                others.append(
                    [
                        beyond[n][0] if layer == 0 else fields[n].get(layer - 1, one[layer - 1]),
                        beyond[n][1] if layer == depth - 1 else fields[n].get(layer + 1, one[layer + 1]),
                    ]
                )
            fed, auto = step_two(fields, outside, layer, others, f_ref[layer], k_ref[layer])
        else:
            fed, auto = fed_mid[layer], auto_mid[layer]
            for end, beside in enumerate((1, depth - 2)):
                if layer == beside:
                    fed = fed + (reach_fast * reach_fast) * far_old[0][end]
                    auto = auto + (reach_slow * reach_slow) * far_old[1][end]
            shading.add(fed, auto, e_ref[layer])
        fed_two[layer] = fed
        auto_two[layer] = auto
    if shading.gather is not None:
        for n, value in enumerate(shading.gather + [shading.before]):
            middle_ref[n] = value


def shade_kernel(depth_count, *refs):
    fed_two, auto_two, e_ref, mix_ref, middle_ref, a_ref, b_ref, corner_ref, fed_out, auto_out, part_ref = refs
    depth, rows, columns = fed_two.shape
    row = lax.broadcasted_iota(jnp.int32, (rows, columns), 0)
    index = lax.axis_index("depth")
    even = is_even("depth")
    there = (
        jnp.logical_and(jnp.logical_not(even), index > 0),
        jnp.logical_and(even, index < depth_count - 1),
    )
    more = []
    for n, reach in enumerate((reach_fast, reach_slow)):
        new_far = sides("depth", (a_ref, b_ref), lambda ref: ref[n])
        above, below = corner_ref[2 * n : 2 * n + 1], corner_ref[2 * n + 1 : 2 * n + 2]
        corner = jnp.where(row == 0, above, 0.0) + jnp.where(row == rows - 1, below, 0.0)
        more.append(
            [reach * new_far[end] + jnp.where(there[end], (2.0 * reach * reach) * corner, 0.0) for end in range(2)]
        )
    shading = Shading(mix_ref)
    for layer in range(depth):
        fed, auto = fed_two[layer], auto_two[layer]
        if layer in (0, depth - 1):
            for end, place in enumerate((0, depth - 1)):
                if layer == place:
                    fed = fed + more[0][end]
                    auto = auto + more[1][end]
            shading.add(fed, auto, e_ref[layer])
        elif layer == 1:
            shading.put([middle_ref[n] for n in range(4)], middle_ref[4])
        fed_out[layer] = fed
        auto_out[layer] = auto
    gather = shading.gather

    block = columns // depth_count
    group = packing(rows, block)
    if not group:
        for channel in range(4):
            part_ref[channel] = gather[channel]
        return
    high = rows // group
    lane = lax.broadcasted_iota(jnp.int32, (high, LANES), 1) // block
    for channel in range(4):
        for tile in range(columns // LANES):
            pieces = [
                gather[channel][q * high : (q + 1) * high, tile * LANES : (tile + 1) * LANES]
                for q in range(group)
            ]
            for p in range(group):
                packed = None
                for q in range(group):
                    turn = (q - p) * block % LANES
                    piece = pltpu.roll(pieces[q], turn, 1) if turn else pieces[q]
                    packed = piece if packed is None else jnp.where(lane == q, piece, packed)
                part_ref[tile * group + p, channel * high : (channel + 1) * high] = packed


def packing(rows, block):
    if block >= LANES or LANES % block:
        return 0
    group = LANES // block
    return group if rows % (group * SUBLANES) == 0 else 0


def last_kernel(group, part_ref, fed_ref, auto_ref, image_out, fed_out, auto_out, image_ref, written):
    copies = [
        pltpu.make_async_copy(ref, out, written.at[n])
        for n, (ref, out) in enumerate(((fed_ref, fed_out), (auto_ref, auto_out), (image_ref, image_out)))
    ]
    copies[0].start()
    copies[1].start()
    _, rows, block = image_ref.shape
    high = rows // group
    count = part_ref.shape[0]
    total = [part_ref[0, channel * high : (channel + 1) * high] for channel in range(4)]
    before = 1.0 - total[3]
    for n in range(1, count):
        for channel in range(4):
            piece = part_ref[n, channel * high : (channel + 1) * high]
            total[channel] = total[channel] + before * piece
        if n < count - 1:
            before = before * (1.0 - piece)
    for channel in range(4):
        for q in range(group):
            image_ref[channel, q * high : (q + 1) * high] = total[channel][:, q * block : (q + 1) * block]
    copies[2].start()
    for copy in copies:
        copy.wait()


def body(substrate, catalyst, feed_rate, kill_rate, extinction, palette):
    depth, rows, columns = substrate.shape
    count = lax.axis_size("depth")
    f32 = functools.partial(jax.ShapeDtypeStruct, dtype=jnp.float32)
    whole = f32(substrate.shape)
    along_depth = pairings("depth", "rows")
    if along_depth[1] is None:
        along_depth[1] = along_depth[0]
    along_rows = [pairs for pairs in pairings("rows", "depth") if pairs is not None]

    cells = (substrate, catalyst, feed_rate, kill_rate)
    pair = f32((2, rows, columns))
    in_hbm = lambda x: pltpu.with_memory_space_constraint(x, pltpu.HBM)
    old_beams = pl.pallas_call(
        old_kernel,
        out_shape=(pair, pair),
        in_specs=[HBM] * 5,
        out_specs=(VMEM,) * 2,
        scratch_shapes=[pltpu.SemaphoreType.DMA((2, 2))],
        cost_estimate=WORK,
        compiler_params=PARAMS,
        name="old_layers",
    )(*(in_hbm(x) for x in (substrate, catalyst, feed_rate, kill_rate, extinction)))
    old_far = [paired(value, pairs) for value, pairs in zip(old_beams[::-1], along_depth)]

    strip = f32((4 * depth, columns))
    outs = pl.pallas_call(
        partial_kernel,
        out_shape=(whole, whole, pair) + (strip,) * len(along_rows),
        in_specs=[VMEM] * 4 + [ANY],
        out_specs=(VMEM,) * (3 + len(along_rows)),
        compiler_params=PARAMS,
        name="partial_step",
    )(*cells, old_beams[0])
    partial = outs[:2]
    new_a = paired(outs[2], along_depth[0])
    beside = [lax.all_gather(value, "rows") for value in outs[3:]]
    *inner, new_b = pl.pallas_call(
        inner_kernel,
        out_shape=(whole,) * 4 + (strip, pair),
        in_specs=[VMEM] * (6 + len(beside)),
        out_specs=(VMEM,) * 6,
        compiler_params=PARAMS,
        name="inner_cells",
    )(*cells, *partial, *beside)
    new_far = [new_a, paired(new_b, along_depth[1])]

    corner = pl.pallas_call(
        functools.partial(corner_kernel, depth),
        out_shape=f32((4, columns)),
        in_specs=[VMEM] * len(beside),
        out_specs=VMEM,
        compiler_params=PARAMS,
        name="corner_rows",
    )(*beside)
    corner = paired(corner, along_depth[0])
    fed, auto, middle, mix = pl.pallas_call(
        second_kernel,
        out_shape=(whole, whole, f32((5, rows, columns)), f32((9, columns))),
        in_specs=[VMEM] * 5 + [SMEM] + [VMEM] * 7,
        out_specs=(VMEM,) * 4,
        cost_estimate=WORK,
        compiler_params=PARAMS,
        name="second_step",
    )(*cells, extinction, palette, *inner, *old_far)

    block = columns // count
    group = packing(rows, block)
    held = pltpu.VMEM(whole.shape, jnp.float32)
    fed, auto, part = pl.pallas_call(
        functools.partial(shade_kernel, count),
        out_shape=(held, held, f32((count, 4 * rows // group, LANES) if group else (4, rows, columns))),
        in_specs=[VMEM] * 8,
        out_specs=(VMEM,) * 3,
        compiler_params=PARAMS,
        name="shading",
    )(fed, auto, extinction, mix, middle, *new_far, corner)
    if not group:
        part = jnp.transpose(part.reshape(4 * rows, count, block), (1, 0, 2))
    part = lax.all_to_all(part, "depth", 0, 0)
    image = f32((4, rows, block))
    image, fed, auto = pl.pallas_call(
        functools.partial(last_kernel, group or 1),
        out_shape=(image, whole, whole),
        in_specs=[VMEM] * 3,
        out_specs=(HBM,) * 3,
        scratch_shapes=[pltpu.VMEM(image.shape, jnp.float32), pltpu.SemaphoreType.DMA((3,))],
        compiler_params=PARAMS,
        name="front_to_back",
    )(part, fed, auto)
    return fed, auto, image


def solution(mesh):
    cells = P("depth", "rows", None)
    return jax.shard_map(
        body,
        mesh=mesh,
        in_specs=(cells,) * 5 + (P(),),
        out_specs=(cells, cells, P(None, "rows", "depth")),
        check_vma=False,
    )
```

```python
import functools

import jax
import jax.numpy as jnp
from jax import lax
from jax.experimental import pallas as pl
from jax.experimental.pallas import tpu as pltpu
from jax.sharding import PartitionSpec as P

diffusion_fast = 0.08
diffusion_slow = 0.04
time_step = 2.0
reach_fast = time_step * diffusion_fast
reach_slow = time_step * diffusion_slow
LANES = 128
SUBLANES = 8
VMEM = pl.BlockSpec(memory_space=pltpu.VMEM)
SMEM = pl.BlockSpec(memory_space=pltpu.SMEM)
HBM = pl.BlockSpec(memory_space=pltpu.HBM)
ANY = pl.BlockSpec(memory_space=pl.ANY)
WORK = pl.CostEstimate(flops=20_000_000, bytes_accessed=4_000_000, transcendentals=0)
PARAMS = pltpu.CompilerParams(vmem_limit_bytes=24 * 1024 * 1024)


def pairings(axis, other):
    count, width = lax.axis_size(axis), lax.axis_size(other)
    flat = (lambda i, j: i * width + j) if axis == "depth" else (lambda i, j: j * count + i)
    result = []
    for shift in (0, 1):
        pairs = []
        for i in range(count):
            partner = ((i + shift) ^ 1) - shift
            for j in range(width):
                if 0 <= partner < count:
                    pairs.append((flat(i, j), flat(partner, j)))
                elif j ^ 1 < width:
                    pairs.append((flat(i, j), flat(i, j ^ 1)))
        result.append(pairs if count > 2 or shift == 0 else None)
    return result


def paired(value, pairs):
    return lax.ppermute(value, ("depth", "rows"), pairs)


def is_even(axis):
    return lax.rem(lax.axis_index(axis), 2) == 0


def partners(axis):
    index, last = lax.axis_index(axis), lax.axis_size(axis) - 1
    odd = lax.rem(index, 2)
    return [jnp.clip(index + 1 - 2 * odd, 0, last), jnp.clip(index - 1 + 2 * odd, 0, last)]


def shifted_columns(value):
    width = value.shape[-1]
    column = lax.broadcasted_iota(jnp.int32, value.shape, value.ndim - 1)
    left = jnp.where(column == 0, 0.0, pltpu.roll(value, 1, value.ndim - 1))
    right = jnp.where(column == width - 1, 0.0, pltpu.roll(value, width - 1, value.ndim - 1))
    return left + right


def shifted_rows(value, above, below):
    rows = value.shape[0]
    row = lax.broadcasted_iota(jnp.int32, value.shape, 0)
    upper = jnp.where(row == 0, above, pltpu.roll(value, 1, 0))
    lower = jnp.where(row == rows - 1, below, pltpu.roll(value, rows - 1, 0))
    return upper + lower


def react(fed, auto, fed_near, auto_near, feed, kill):
    reaction = fed * auto * auto
    fed_change = diffusion_fast * (fed_near - 6.0 * fed) - reaction + feed * (1.0 - fed)
    auto_change = diffusion_slow * (auto_near - 6.0 * auto) + reaction - (feed + kill) * auto
    return fed + time_step * fed_change, auto + time_step * auto_change


def partial_step(s_ref, c_ref, feed, kill, layer, inner):
    near = []
    for ref in (s_ref, c_ref):
        value = ref[layer]
        total = shifted_rows(value, 0.0, 0.0) + shifted_columns(value)
        for other in inner:
            total = total + ref[other]
        near.append(total)
    return react(s_ref[layer], c_ref[layer], near[0], near[1], feed, kill)


def old_kernel(s_hbm, c_hbm, *refs):
    b_ref, a_ref, arrived = refs[-3:]
    depth = s_hbm.shape[0]
    even = is_even("depth")
    copies = []
    for n, (out, towards_next) in enumerate(((a_ref, even), (b_ref, jnp.logical_not(even)))):
        layer = jnp.where(towards_next, depth - 1, 0)
        for i, hbm in enumerate((s_hbm, c_hbm)):
            copies.append(pltpu.make_async_copy(hbm.at[layer], out.at[i], arrived.at[n, i]))
    for copy in copies:
        copy.start()
    for copy in copies:
        copy.wait()


def partial_kernel(s_ref, c_ref, f_ref, k_ref, _, ps_ref, pc_ref, a_ref, *strips):
    depth, rows, _ = s_ref.shape
    for layer in range(depth):
        inner = [other for other in (layer - 1, layer + 1) if 0 <= other < depth]
        ps_ref[layer], pc_ref[layer] = partial_step(s_ref, c_ref, f_ref[layer], k_ref[layer], layer, inner)
    layer = jnp.where(is_even("depth"), depth - 1, 0)
    a_ref[0] = ps_ref[layer]
    a_ref[1] = pc_ref[layer]
    even = is_even("rows")
    for out, towards_next in zip(strips, (even, jnp.logical_not(even))):
        for n, ref in enumerate((s_ref, c_ref, ps_ref, pc_ref)):
            for layer in range(depth):
                head, tail = ref[layer, 0:1], ref[layer, rows - 1 : rows]
                out[n * depth + layer : n * depth + layer + 1] = jnp.where(towards_next, tail, head)


def sides(axis, refs, read):
    index, count = lax.axis_index(axis), lax.axis_size(axis)
    even = is_even(axis)
    first = read(refs[0])
    second = read(refs[1]) if len(refs) == 2 else 0.0
    before = jnp.where(even, second, first)
    after = jnp.where(even, first, second)
    return jnp.where(index == 0, 0.0, before), jnp.where(index == count - 1, 0.0, after)


def step_two(fields, outside, layer, others, feed, kill):
    near = []
    for n in range(2):
        value = fields[n][layer]
        total = shifted_rows(value, outside[n][layer][0], outside[n][layer][1]) + shifted_columns(value)
        for other in others[n]:
            total = total + other
        near.append(total)
    return react(fields[0][layer], fields[1][layer], near[0], near[1], feed, kill)


def inner_kernel(s_ref, c_ref, f_ref, k_ref, ps_ref, pc_ref, *refs):
    *strips, fed_one, auto_one, fed_two, auto_two, outer_ref, b_ref = refs
    beside = [ref.at[place] for ref, place in zip(strips, partners("rows"))]
    depth, rows, columns = s_ref.shape
    row = lax.broadcasted_iota(jnp.int32, (rows, columns), 0)
    index, last = lax.axis_index("rows"), lax.axis_size("rows") - 1
    inside = (index > 0, index < last)
    fields, outside = [], []
    for n, (old, partial, out, reach) in enumerate(
        ((s_ref, ps_ref, fed_one, reach_fast), (c_ref, pc_ref, auto_one, reach_slow))
    ):
        values, rows_outside = [], []
        for layer in range(depth):
            at = n * depth + layer
            above, below = sides("rows", beside, lambda ref: ref[at : at + 1])
            near = jnp.where(row == 0, above, 0.0) + jnp.where(row == rows - 1, below, 0.0)
            value = partial[layer] + reach * near
            values.append(value)
            out[layer] = value
            at = (2 + n) * depth + layer
            beyond = sides("rows", beside, lambda ref: ref[at : at + 1])
            ends = []
            for side, own in enumerate((old[layer, 0:1], old[layer, rows - 1 : rows])):
                end = jnp.where(inside[side], beyond[side] + reach * own, 0.0)
                ends.append(end)
                at = (n * 2 + side) * depth + layer
                outer_ref[at : at + 1] = end
            rows_outside.append(ends)
        fields.append(values)
        outside.append(rows_outside)
    for layer in range(1, depth - 1):
        others = [(values[layer - 1], values[layer + 1]) for values in fields]
        fed_two[layer], auto_two[layer] = step_two(fields, outside, layer, others, f_ref[layer], k_ref[layer])
    end = jnp.where(is_even("depth"), 0, depth - 1)
    for n, (one, partial) in enumerate(((fed_one, ps_ref), (auto_one, pc_ref))):
        b_ref[n] = one[end] + (one[end] - partial[end])


def corner_kernel(depth, *refs):
    *strips, out = refs
    beside = [ref.at[place] for ref, place in zip(strips, partners("rows"))]
    even = is_even("depth")
    for n in range(2):
        first, final = [
            sides("rows", beside, lambda ref: ref[n * depth + layer : n * depth + layer + 1])
            for layer in (0, depth - 1)
        ]
        for side in range(2):
            out[2 * n + side : 2 * n + side + 1] = jnp.where(even, final[side], first[side])


class Shading:
    def __init__(self, mix_ref):
        self.mix = [[mix_ref[3 * k + n : 3 * k + n + 1] for n in range(3)] for k in range(3)]
        self.gather = None
        self.before = None

    def put(self, pieces, passing):
        if self.gather is None:
            self.gather, self.before = list(pieces), passing
            return
        self.gather = [total + self.before * piece for total, piece in zip(self.gather, pieces)]
        self.before = self.before * passing

    def add(self, fed, auto, extinction):
        passing = jnp.exp(-extinction * (0.25 + 4.0 * auto * auto))
        opacity = 1.0 - passing
        half = 0.5 * opacity
        pieces = []
        for fed_mix, auto_mix, offset in self.mix:
            level = fed_mix * (fed - 0.65) + auto_mix * (auto - 0.25) + offset
            pieces.append(half + half * jnp.tanh(level))
        self.put(pieces + [opacity], passing)


def second_kernel(*refs):
    s_ref, c_ref, f_ref, k_ref, e_ref, palette = refs[:6]
    fed_one, auto_one, fed_mid, auto_mid, outer_ref = refs[6:11]
    far = refs[11:13]
    fed_two, auto_two, middle_ref, mix_ref = refs[13:]
    for channel in range(3):
        for n, scale in enumerate((4.0, 4.0, 0.5)):
            at = 3 * channel + n
            mix_ref[at : at + 1] = jnp.full((1, s_ref.shape[2]), scale * palette[channel, n], jnp.float32)
    depth = s_ref.shape[0]
    index, last = lax.axis_index("depth"), lax.axis_size("depth") - 1
    inside = (index > 0, index < last)
    ends = (0, depth - 1)
    fields, outside, beyond, far_old = [], [], [], []
    for n, (old, one, reach) in enumerate(((s_ref, fed_one, reach_fast), (c_ref, auto_one, reach_slow))):
        old_far = sides("depth", far, lambda ref: ref[n])
        far_old.append(old_far)
        beyond.append([])
        values, rows_outside = {}, {}
        for end, layer in enumerate(ends):
            beyond[n].append(jnp.where(inside[end], reach * old[layer], 0.0))
        for layer in set(ends):
            near = 0.0
            for end in range(2):
                if layer == ends[end]:
                    near = near + old_far[end]
            values[layer] = one[layer] + reach * near
            rows_outside[layer] = [
                outer_ref[(n * 2 + side) * depth + layer : (n * 2 + side) * depth + layer + 1] for side in range(2)
            ]
        fields.append(values)
        outside.append(rows_outside)
    shading = Shading(mix_ref)
    for layer in range(depth):
        if layer in ends:
            others = []
            for n, one in enumerate((fed_one, auto_one)):
                others.append(
                    [
                        beyond[n][0] if layer == 0 else fields[n].get(layer - 1, one[layer - 1]),
                        beyond[n][1] if layer == depth - 1 else fields[n].get(layer + 1, one[layer + 1]),
                    ]
                )
            fed, auto = step_two(fields, outside, layer, others, f_ref[layer], k_ref[layer])
        else:
            fed, auto = fed_mid[layer], auto_mid[layer]
            for end, beside in enumerate((1, depth - 2)):
                if layer == beside:
                    fed = fed + (reach_fast * reach_fast) * far_old[0][end]
                    auto = auto + (reach_slow * reach_slow) * far_old[1][end]
            shading.add(fed, auto, e_ref[layer])
        fed_two[layer] = fed
        auto_two[layer] = auto
    if shading.gather is not None:
        for n, value in enumerate(shading.gather + [shading.before]):
            middle_ref[n] = value


def shade_kernel(depth_count, *refs):
    fed_two, auto_two, e_ref, mix_ref, middle_ref, a_ref, b_ref, corner_ref, fed_out, auto_out, part_ref = refs
    depth, rows, columns = fed_two.shape
    row = lax.broadcasted_iota(jnp.int32, (rows, columns), 0)
    index = lax.axis_index("depth")
    even = is_even("depth")
    there = (
        jnp.logical_and(jnp.logical_not(even), index > 0),
        jnp.logical_and(even, index < depth_count - 1),
    )
    more = []
    for n, reach in enumerate((reach_fast, reach_slow)):
        new_far = sides("depth", (a_ref, b_ref), lambda ref: ref[n])
        above, below = corner_ref[2 * n : 2 * n + 1], corner_ref[2 * n + 1 : 2 * n + 2]
        corner = jnp.where(row == 0, above, 0.0) + jnp.where(row == rows - 1, below, 0.0)
        more.append(
            [reach * new_far[end] + jnp.where(there[end], (2.0 * reach * reach) * corner, 0.0) for end in range(2)]
        )
    shading = Shading(mix_ref)
    for layer in range(depth):
        fed, auto = fed_two[layer], auto_two[layer]
        if layer in (0, depth - 1):
            for end, place in enumerate((0, depth - 1)):
                if layer == place:
                    fed = fed + more[0][end]
                    auto = auto + more[1][end]
            shading.add(fed, auto, e_ref[layer])
        elif layer == 1:
            shading.put([middle_ref[n] for n in range(4)], middle_ref[4])
        fed_out[layer] = fed
        auto_out[layer] = auto
    gather = shading.gather

    block = columns // depth_count
    group = packing(rows, block)
    if not group:
        for channel in range(4):
            part_ref[channel] = gather[channel]
        return
    high = rows // group
    lane = lax.broadcasted_iota(jnp.int32, (high, LANES), 1) // block
    for channel in range(4):
        for tile in range(columns // LANES):
            pieces = [
                gather[channel][q * high : (q + 1) * high, tile * LANES : (tile + 1) * LANES]
                for q in range(group)
            ]
            for p in range(group):
                packed = None
                for q in range(group):
                    turn = (q - p) * block % LANES
                    piece = pltpu.roll(pieces[q], turn, 1) if turn else pieces[q]
                    packed = piece if packed is None else jnp.where(lane == q, piece, packed)
                part_ref[tile * group + p, channel * high : (channel + 1) * high] = packed


def packing(rows, block):
    if block >= LANES or LANES % block:
        return 0
    group = LANES // block
    return group if rows % (group * SUBLANES) == 0 else 0


def last_kernel(group, part_ref, fed_ref, auto_ref, image_out, fed_out, auto_out, image_ref, written):
    copies = [
        pltpu.make_async_copy(ref, out, written.at[n])
        for n, (ref, out) in enumerate(((fed_ref, fed_out), (auto_ref, auto_out), (image_ref, image_out)))
    ]
    copies[0].start()
    copies[1].start()
    _, rows, block = image_ref.shape
    high = rows // group
    count = part_ref.shape[0]
    total = [part_ref[0, channel * high : (channel + 1) * high] for channel in range(4)]
    before = 1.0 - total[3]
    for n in range(1, count):
        for channel in range(4):
            piece = part_ref[n, channel * high : (channel + 1) * high]
            total[channel] = total[channel] + before * piece
        if n < count - 1:
            before = before * (1.0 - piece)
    for channel in range(4):
        for q in range(group):
            image_ref[channel, q * high : (q + 1) * high] = total[channel][:, q * block : (q + 1) * block]
    copies[2].start()
    for copy in copies:
        copy.wait()


def body(substrate, catalyst, feed_rate, kill_rate, extinction, palette):
    depth, rows, columns = substrate.shape
    count = lax.axis_size("depth")
    f32 = functools.partial(jax.ShapeDtypeStruct, dtype=jnp.float32)
    whole = f32(substrate.shape)
    along_depth = pairings("depth", "rows")
    if along_depth[1] is None:
        along_depth[1] = along_depth[0]
    along_rows = [pairs for pairs in pairings("rows", "depth") if pairs is not None]

    cells = (substrate, catalyst, feed_rate, kill_rate)
    pair = f32((2, rows, columns))
    in_hbm = lambda x: pltpu.with_memory_space_constraint(x, pltpu.HBM)
    old_beams = pl.pallas_call(
        old_kernel,
        out_shape=(pair, pair),
        in_specs=[HBM] * 5,
        out_specs=(VMEM,) * 2,
        scratch_shapes=[pltpu.SemaphoreType.DMA((2, 2))],
        cost_estimate=WORK,
        compiler_params=PARAMS,
        name="old_layers",
    )(*(in_hbm(x) for x in (substrate, catalyst, feed_rate, kill_rate, extinction)))
    old_far = [paired(value, pairs) for value, pairs in zip(old_beams[::-1], along_depth)]

    strip = f32((4 * depth, columns))
    outs = pl.pallas_call(
        partial_kernel,
        out_shape=(whole, whole, pair) + (strip,) * len(along_rows),
        in_specs=[VMEM] * 4 + [ANY],
        out_specs=(VMEM,) * (3 + len(along_rows)),
        compiler_params=PARAMS,
        name="partial_step",
    )(*cells, old_beams[0])
    partial = outs[:2]
    new_a = paired(outs[2], along_depth[0])
    beside = [lax.all_gather(value, "rows") for value in outs[3:]]
    *inner, new_b = pl.pallas_call(
        inner_kernel,
        out_shape=(whole,) * 4 + (strip, pair),
        in_specs=[VMEM] * (6 + len(beside)),
        out_specs=(VMEM,) * 6,
        compiler_params=PARAMS,
        name="inner_cells",
    )(*cells, *partial, *beside)
    new_far = [new_a, paired(new_b, along_depth[1])]

    corner = pl.pallas_call(
        functools.partial(corner_kernel, depth),
        out_shape=f32((4, columns)),
        in_specs=[VMEM] * len(beside),
        out_specs=VMEM,
        compiler_params=PARAMS,
        name="corner_rows",
    )(*beside)
    corner = paired(corner, along_depth[0])
    fed, auto, middle, mix = pl.pallas_call(
        second_kernel,
        out_shape=(whole, whole, f32((5, rows, columns)), f32((9, columns))),
        in_specs=[VMEM] * 5 + [SMEM] + [VMEM] * 7,
        out_specs=(VMEM,) * 4,
        cost_estimate=WORK,
        compiler_params=PARAMS,
        name="second_step",
    )(*cells, extinction, palette, *inner, *old_far)

    block = columns // count
    group = packing(rows, block)
    held = pltpu.VMEM(whole.shape, jnp.float32)
    fed, auto, part = pl.pallas_call(
        functools.partial(shade_kernel, count),
        out_shape=(held, held, f32((count, 4 * rows // group, LANES) if group else (4, rows, columns))),
        in_specs=[VMEM] * 8,
        out_specs=(VMEM,) * 3,
        compiler_params=PARAMS,
        name="shading",
    )(fed, auto, extinction, mix, middle, *new_far, corner)
    if not group:
        part = jnp.transpose(part.reshape(4 * rows, count, block), (1, 0, 2))
    part = lax.all_to_all(part, "depth", 0, 0)
    image = f32((4, rows, block))
    image, fed, auto = pl.pallas_call(
        functools.partial(last_kernel, group or 1),
        out_shape=(image, whole, whole),
        in_specs=[VMEM] * 3,
        out_specs=(HBM,) * 3,
        scratch_shapes=[pltpu.VMEM(image.shape, jnp.float32), pltpu.SemaphoreType.DMA((3,))],
        compiler_params=PARAMS,
        name="front_to_back",
    )(part, fed, auto)
    return fed, auto, image


def solution(mesh):
    cells = P("depth", "rows", None)
    return jax.shard_map(
        body,
        mesh=mesh,
        in_specs=(cells,) * 5 + (P(),),
        out_specs=(cells, cells, P(None, "rows", "depth")),
        check_vma=False,
    )
```

```python
import functools

import jax
import jax.numpy as jnp
from jax import lax
from jax.experimental import pallas as pl
from jax.experimental.pallas import tpu as pltpu
from jax.sharding import PartitionSpec as P

diffusion_fast = 0.08
diffusion_slow = 0.04
time_step = 2.0
reach_fast = time_step * diffusion_fast
reach_slow = time_step * diffusion_slow
LANES = 128
SUBLANES = 8
VMEM = pl.BlockSpec(memory_space=pltpu.VMEM)
SMEM = pl.BlockSpec(memory_space=pltpu.SMEM)
HBM = pl.BlockSpec(memory_space=pltpu.HBM)
ANY = pl.BlockSpec(memory_space=pl.ANY)
WORK = pl.CostEstimate(flops=20_000_000, bytes_accessed=4_000_000, transcendentals=0)
PARAMS = pltpu.CompilerParams(vmem_limit_bytes=24 * 1024 * 1024)


def pairings(axis, other):
    count, width = lax.axis_size(axis), lax.axis_size(other)
    flat = (lambda i, j: i * width + j) if axis == "depth" else (lambda i, j: j * count + i)
    result = []
    for shift in (0, 1):
        pairs = []
        for i in range(count):
            partner = ((i + shift) ^ 1) - shift
            for j in range(width):
                if 0 <= partner < count:
                    pairs.append((flat(i, j), flat(partner, j)))
                elif j ^ 1 < width:
                    pairs.append((flat(i, j), flat(i, j ^ 1)))
        result.append(pairs if count > 2 or shift == 0 else None)
    return result


def paired(value, pairs):
    return lax.ppermute(value, ("depth", "rows"), pairs)


def is_even(axis):
    return lax.rem(lax.axis_index(axis), 2) == 0


def partners(axis):
    index, last = lax.axis_index(axis), lax.axis_size(axis) - 1
    odd = lax.rem(index, 2)
    return [jnp.clip(index + 1 - 2 * odd, 0, last), jnp.clip(index - 1 + 2 * odd, 0, last)]


def shifted_columns(value):
    width = value.shape[-1]
    column = lax.broadcasted_iota(jnp.int32, value.shape, value.ndim - 1)
    left = jnp.where(column == 0, 0.0, pltpu.roll(value, 1, value.ndim - 1))
    right = jnp.where(column == width - 1, 0.0, pltpu.roll(value, width - 1, value.ndim - 1))
    return left + right


def shifted_rows(value, above, below):
    rows = value.shape[0]
    row = lax.broadcasted_iota(jnp.int32, value.shape, 0)
    upper = jnp.where(row == 0, above, pltpu.roll(value, 1, 0))
    lower = jnp.where(row == rows - 1, below, pltpu.roll(value, rows - 1, 0))
    return upper + lower


def react(fed, auto, fed_near, auto_near, feed, kill):
    reaction = fed * auto * auto
    fed_change = diffusion_fast * (fed_near - 6.0 * fed) - reaction + feed * (1.0 - fed)
    auto_change = diffusion_slow * (auto_near - 6.0 * auto) + reaction - (feed + kill) * auto
    return fed + time_step * fed_change, auto + time_step * auto_change


def partial_step(s_ref, c_ref, feed, kill, layer, inner):
    near = []
    for ref in (s_ref, c_ref):
        value = ref[layer]
        total = shifted_rows(value, 0.0, 0.0) + shifted_columns(value)
        for other in inner:
            total = total + ref[other]
        near.append(total)
    return react(s_ref[layer], c_ref[layer], near[0], near[1], feed, kill)


def old_kernel(s_hbm, c_hbm, *refs):
    b_ref, a_ref, arrived = refs[-3:]
    depth, rows, _ = s_hbm.shape
    cuts = 2 if rows % (2 * SUBLANES) == 0 else 1
    even = is_even("depth")
    copies = []
    for n, (out, towards_next) in enumerate(((a_ref, even), (b_ref, jnp.logical_not(even)))):
        layer = jnp.where(towards_next, depth - 1, 0)
        for i, hbm in enumerate((s_hbm, c_hbm)):
            for k in range(cuts):
                part = pl.ds(k * (rows // cuts), rows // cuts)
                copies.append(pltpu.make_async_copy(hbm.at[layer, part], out.at[i, part], arrived.at[n, cuts * i + k]))
    for copy in copies:
        copy.start()
    for copy in copies:
        copy.wait()


def partial_kernel(s_ref, c_ref, f_ref, k_ref, _, ps_ref, pc_ref, a_ref, *strips):
    depth, rows, _ = s_ref.shape
    for layer in range(depth):
        inner = [other for other in (layer - 1, layer + 1) if 0 <= other < depth]
        ps_ref[layer], pc_ref[layer] = partial_step(s_ref, c_ref, f_ref[layer], k_ref[layer], layer, inner)
    layer = jnp.where(is_even("depth"), depth - 1, 0)
    a_ref[0] = ps_ref[layer]
    a_ref[1] = pc_ref[layer]
    even = is_even("rows")
    for out, towards_next in zip(strips, (even, jnp.logical_not(even))):
        for n, ref in enumerate((s_ref, c_ref, ps_ref, pc_ref)):
            for layer in range(depth):
                head, tail = ref[layer, 0:1], ref[layer, rows - 1 : rows]
                out[n * depth + layer : n * depth + layer + 1] = jnp.where(towards_next, tail, head)


def sides(axis, refs, read):
    index, count = lax.axis_index(axis), lax.axis_size(axis)
    even = is_even(axis)
    first = read(refs[0])
    second = read(refs[1]) if len(refs) == 2 else 0.0
    before = jnp.where(even, second, first)
    after = jnp.where(even, first, second)
    return jnp.where(index == 0, 0.0, before), jnp.where(index == count - 1, 0.0, after)


def step_two(fields, outside, layer, others, feed, kill):
    near = []
    for n in range(2):
        value = fields[n][layer]
        total = shifted_rows(value, outside[n][layer][0], outside[n][layer][1]) + shifted_columns(value)
        for other in others[n]:
            total = total + other
        near.append(total)
    return react(fields[0][layer], fields[1][layer], near[0], near[1], feed, kill)


def inner_kernel(s_ref, c_ref, f_ref, k_ref, ps_ref, pc_ref, *refs):
    *strips, fed_one, auto_one, fed_two, auto_two, outer_ref, b_ref = refs
    beside = [ref.at[place] for ref, place in zip(strips, partners("rows"))]
    depth, rows, columns = s_ref.shape
    row = lax.broadcasted_iota(jnp.int32, (rows, columns), 0)
    index, last = lax.axis_index("rows"), lax.axis_size("rows") - 1
    inside = (index > 0, index < last)
    fields, outside = [], []
    for n, (old, partial, out, reach) in enumerate(
        ((s_ref, ps_ref, fed_one, reach_fast), (c_ref, pc_ref, auto_one, reach_slow))
    ):
        values, rows_outside = [], []
        for layer in range(depth):
            at = n * depth + layer
            above, below = sides("rows", beside, lambda ref: ref[at : at + 1])
            near = jnp.where(row == 0, above, 0.0) + jnp.where(row == rows - 1, below, 0.0)
            value = partial[layer] + reach * near
            values.append(value)
            out[layer] = value
            at = (2 + n) * depth + layer
            beyond = sides("rows", beside, lambda ref: ref[at : at + 1])
            ends = []
            for side, own in enumerate((old[layer, 0:1], old[layer, rows - 1 : rows])):
                end = jnp.where(inside[side], beyond[side] + reach * own, 0.0)
                ends.append(end)
                at = (n * 2 + side) * depth + layer
                outer_ref[at : at + 1] = end
            rows_outside.append(ends)
        fields.append(values)
        outside.append(rows_outside)
    for layer in range(1, depth - 1):
        others = [(values[layer - 1], values[layer + 1]) for values in fields]
        fed_two[layer], auto_two[layer] = step_two(fields, outside, layer, others, f_ref[layer], k_ref[layer])
    end = jnp.where(is_even("depth"), 0, depth - 1)
    for n, (one, partial) in enumerate(((fed_one, ps_ref), (auto_one, pc_ref))):
        b_ref[n] = one[end] + (one[end] - partial[end])


def corner_kernel(depth, *refs):
    *strips, out = refs
    beside = [ref.at[place] for ref, place in zip(strips, partners("rows"))]
    even = is_even("depth")
    for n in range(2):
        first, final = [
            sides("rows", beside, lambda ref: ref[n * depth + layer : n * depth + layer + 1])
            for layer in (0, depth - 1)
        ]
        for side in range(2):
            out[2 * n + side : 2 * n + side + 1] = jnp.where(even, final[side], first[side])


class Shading:
    def __init__(self, mix_ref):
        self.mix = [[mix_ref[3 * k + n : 3 * k + n + 1] for n in range(3)] for k in range(3)]
        self.gather = None
        self.before = None

    def put(self, pieces, passing):
        if self.gather is None:
            self.gather, self.before = list(pieces), passing
            return
        self.gather = [total + self.before * piece for total, piece in zip(self.gather, pieces)]
        self.before = self.before * passing

    def add(self, fed, auto, extinction):
        passing = jnp.exp(-extinction * (0.25 + 4.0 * auto * auto))
        opacity = 1.0 - passing
        pieces = []
        for fed_mix, auto_mix, offset in self.mix:
            level = fed_mix * (fed - 0.65) + auto_mix * (auto - 0.25) + offset
            pieces.append(opacity / (1.0 + jnp.exp(-level)))
        self.put(pieces + [opacity], passing)


def second_kernel(*refs):
    s_ref, c_ref, f_ref, k_ref, e_ref, palette = refs[:6]
    fed_one, auto_one, fed_mid, auto_mid, outer_ref = refs[6:11]
    far = refs[11:13]
    fed_two, auto_two, middle_ref, mix_ref = refs[13:]
    for channel in range(3):
        for n, scale in enumerate((8.0, 8.0, 1.0)):
            at = 3 * channel + n
            mix_ref[at : at + 1] = jnp.full((1, s_ref.shape[2]), scale * palette[channel, n], jnp.float32)
    depth = s_ref.shape[0]
    index, last = lax.axis_index("depth"), lax.axis_size("depth") - 1
    inside = (index > 0, index < last)
    ends = (0, depth - 1)
    fields, outside, beyond, far_old = [], [], [], []
    for n, (old, one, reach) in enumerate(((s_ref, fed_one, reach_fast), (c_ref, auto_one, reach_slow))):
        old_far = sides("depth", far, lambda ref: ref[n])
        far_old.append(old_far)
        beyond.append([])
        values, rows_outside = {}, {}
        for end, layer in enumerate(ends):
            beyond[n].append(jnp.where(inside[end], reach * old[layer], 0.0))
        for layer in set(ends):
            near = 0.0
            for end in range(2):
                if layer == ends[end]:
                    near = near + old_far[end]
            values[layer] = one[layer] + reach * near
            rows_outside[layer] = [
                outer_ref[(n * 2 + side) * depth + layer : (n * 2 + side) * depth + layer + 1] for side in range(2)
            ]
        fields.append(values)
        outside.append(rows_outside)
    shading = Shading(mix_ref)
    for layer in range(depth):
        if layer in ends:
            others = []
            for n, one in enumerate((fed_one, auto_one)):
                others.append(
                    [
                        beyond[n][0] if layer == 0 else fields[n].get(layer - 1, one[layer - 1]),
                        beyond[n][1] if layer == depth - 1 else fields[n].get(layer + 1, one[layer + 1]),
                    ]
                )
            fed, auto = step_two(fields, outside, layer, others, f_ref[layer], k_ref[layer])
        else:
            fed, auto = fed_mid[layer], auto_mid[layer]
            for end, beside in enumerate((1, depth - 2)):
                if layer == beside:
                    fed = fed + (reach_fast * reach_fast) * far_old[0][end]
                    auto = auto + (reach_slow * reach_slow) * far_old[1][end]
            shading.add(fed, auto, e_ref[layer])
        fed_two[layer] = fed
        auto_two[layer] = auto
    if shading.gather is not None:
        for n, value in enumerate(shading.gather + [shading.before]):
            middle_ref[n] = value


def shade_kernel(depth_count, *refs):
    fed_two, auto_two, e_ref, mix_ref, middle_ref, a_ref, b_ref, corner_ref, fed_out, auto_out, part_ref = refs
    depth, rows, columns = fed_two.shape
    row = lax.broadcasted_iota(jnp.int32, (rows, columns), 0)
    index = lax.axis_index("depth")
    even = is_even("depth")
    there = (
        jnp.logical_and(jnp.logical_not(even), index > 0),
        jnp.logical_and(even, index < depth_count - 1),
    )
    more = []
    for n, reach in enumerate((reach_fast, reach_slow)):
        new_far = sides("depth", (a_ref, b_ref), lambda ref: ref[n])
        above, below = corner_ref[2 * n : 2 * n + 1], corner_ref[2 * n + 1 : 2 * n + 2]
        corner = jnp.where(row == 0, above, 0.0) + jnp.where(row == rows - 1, below, 0.0)
        more.append(
            [reach * new_far[end] + jnp.where(there[end], (2.0 * reach * reach) * corner, 0.0) for end in range(2)]
        )
    shading = Shading(mix_ref)
    for layer in range(depth):
        fed, auto = fed_two[layer], auto_two[layer]
        if layer in (0, depth - 1):
            for end, place in enumerate((0, depth - 1)):
                if layer == place:
                    fed = fed + more[0][end]
                    auto = auto + more[1][end]
            shading.add(fed, auto, e_ref[layer])
        elif layer == 1:
            shading.put([middle_ref[n] for n in range(4)], middle_ref[4])
        fed_out[layer] = fed
        auto_out[layer] = auto
    gather = shading.gather

    block = columns // depth_count
    group = packing(rows, block)
    if not group:
        for channel in range(4):
            part_ref[channel] = gather[channel]
        return
    high = rows // group
    lane = lax.broadcasted_iota(jnp.int32, (high, LANES), 1) // block
    for channel in range(4):
        for tile in range(columns // LANES):
            pieces = [
                gather[channel][q * high : (q + 1) * high, tile * LANES : (tile + 1) * LANES]
                for q in range(group)
            ]
            for p in range(group):
                packed = None
                for q in range(group):
                    turn = (q - p) * block % LANES
                    piece = pltpu.roll(pieces[q], turn, 1) if turn else pieces[q]
                    packed = piece if packed is None else jnp.where(lane == q, piece, packed)
                part_ref[tile * group + p, channel * high : (channel + 1) * high] = packed


def packing(rows, block):
    if block >= LANES or LANES % block:
        return 0
    group = LANES // block
    return group if rows % (group * SUBLANES) == 0 else 0


def last_kernel(group, part_ref, fed_ref, auto_ref, image_out, fed_out, auto_out, image_ref, written):
    copies = [
        pltpu.make_async_copy(ref, out, written.at[n])
        for n, (ref, out) in enumerate(((fed_ref, fed_out), (auto_ref, auto_out), (image_ref, image_out)))
    ]
    copies[0].start()
    copies[1].start()
    _, rows, block = image_ref.shape
    high = rows // group
    count = part_ref.shape[0]
    total = [part_ref[0, channel * high : (channel + 1) * high] for channel in range(4)]
    before = 1.0 - total[3]
    for n in range(1, count):
        for channel in range(4):
            piece = part_ref[n, channel * high : (channel + 1) * high]
            total[channel] = total[channel] + before * piece
        if n < count - 1:
            before = before * (1.0 - piece)
    for channel in range(4):
        for q in range(group):
            image_ref[channel, q * high : (q + 1) * high] = total[channel][:, q * block : (q + 1) * block]
    copies[2].start()
    for copy in copies:
        copy.wait()


def body(substrate, catalyst, feed_rate, kill_rate, extinction, palette):
    depth, rows, columns = substrate.shape
    count = lax.axis_size("depth")
    f32 = functools.partial(jax.ShapeDtypeStruct, dtype=jnp.float32)
    whole = f32(substrate.shape)
    along_depth = pairings("depth", "rows")
    if along_depth[1] is None:
        along_depth[1] = along_depth[0]
    along_rows = [pairs for pairs in pairings("rows", "depth") if pairs is not None]

    cells = (substrate, catalyst, feed_rate, kill_rate)
    pair = f32((2, rows, columns))
    in_hbm = lambda x: pltpu.with_memory_space_constraint(x, pltpu.HBM)
    old_beams = pl.pallas_call(
        old_kernel,
        out_shape=(pair, pair),
        in_specs=[HBM] * 5,
        out_specs=(VMEM,) * 2,
        scratch_shapes=[pltpu.SemaphoreType.DMA((2, 4))],
        cost_estimate=WORK,
        compiler_params=PARAMS,
        name="old_layers",
    )(*(in_hbm(x) for x in (substrate, catalyst, feed_rate, kill_rate, extinction)))
    old_far = [paired(value, pairs) for value, pairs in zip(old_beams[::-1], along_depth)]

    strip = f32((4 * depth, columns))
    outs = pl.pallas_call(
        partial_kernel,
        out_shape=(whole, whole, pair) + (strip,) * len(along_rows),
        in_specs=[VMEM] * 4 + [ANY],
        out_specs=(VMEM,) * (3 + len(along_rows)),
        compiler_params=PARAMS,
        name="partial_step",
    )(*cells, old_beams[0])
    partial = outs[:2]
    new_a = paired(outs[2], along_depth[0])
    beside = [lax.all_gather(value, "rows") for value in outs[3:]]
    *inner, new_b = pl.pallas_call(
        inner_kernel,
        out_shape=(whole,) * 4 + (strip, pair),
        in_specs=[VMEM] * (6 + len(beside)),
        out_specs=(VMEM,) * 6,
        compiler_params=PARAMS,
        name="inner_cells",
    )(*cells, *partial, *beside)
    new_far = [new_a, paired(new_b, along_depth[1])]

    corner = pl.pallas_call(
        functools.partial(corner_kernel, depth),
        out_shape=f32((4, columns)),
        in_specs=[VMEM] * len(beside),
        out_specs=VMEM,
        compiler_params=PARAMS,
        name="corner_rows",
    )(*beside)
    corner = paired(corner, along_depth[0])
    fed, auto, middle, mix = pl.pallas_call(
        second_kernel,
        out_shape=(whole, whole, f32((5, rows, columns)), f32((9, columns))),
        in_specs=[VMEM] * 5 + [SMEM] + [VMEM] * 7,
        out_specs=(VMEM,) * 4,
        cost_estimate=WORK,
        compiler_params=PARAMS,
        name="second_step",
    )(*cells, extinction, palette, *inner, *old_far)

    block = columns // count
    group = packing(rows, block)
    held = pltpu.VMEM(whole.shape, jnp.float32)
    fed, auto, part = pl.pallas_call(
        functools.partial(shade_kernel, count),
        out_shape=(held, held, f32((count, 4 * rows // group, LANES) if group else (4, rows, columns))),
        in_specs=[VMEM] * 8,
        out_specs=(VMEM,) * 3,
        compiler_params=PARAMS,
        name="shading",
    )(fed, auto, extinction, mix, middle, *new_far, corner)
    if not group:
        part = jnp.transpose(part.reshape(4 * rows, count, block), (1, 0, 2))
    part = lax.all_to_all(part, "depth", 0, 0)
    image = f32((4, rows, block))
    image, fed, auto = pl.pallas_call(
        functools.partial(last_kernel, group or 1),
        out_shape=(image, whole, whole),
        in_specs=[VMEM] * 3,
        out_specs=(HBM,) * 3,
        scratch_shapes=[pltpu.VMEM(image.shape, jnp.float32), pltpu.SemaphoreType.DMA((3,))],
        compiler_params=PARAMS,
        name="front_to_back",
    )(part, fed, auto)
    return fed, auto, image


def solution(mesh):
    cells = P("depth", "rows", None)
    return jax.shard_map(
        body,
        mesh=mesh,
        in_specs=(cells,) * 5 + (P(),),
        out_specs=(cells, cells, P(None, "rows", "depth")),
        check_vma=False,
    )
```
